512 devices in a mesh: row: 64 (over x, z), col: 8 (over y, core).
Axes of the slice: x: 4, y: 4, z: 16, core: 2. Of those that a mesh axis runs over, the one named last changes fastest.
Arguments:
- slab_rows: float32 [131072, 1024], P('row', 'col')
- row_flips: int32 [131072], P('row'), may hold values from 0 to 1
- sample_holder: int32 [8192, 1], P('row'), may hold values from 0 to 63; in each aligned block of 128 rows (0 to 127, 128 to 255, ...) at most 4 rows name the same one
- sample_offset: int32 [8192], P('row'), may hold values from 0 to 2047
Outputs:
- mixed_slab: float32 [131072, 1024], P('row', 'col')
- precond: float32 [1024, 1024], P(None, 'col')
The draws below stay inside these ranges and needn't reach their ends.
Inputs may be any that keep to these rules, and one draw needn't show every extreme that they name: `sample_holder`: each owner's list of 128 entries names no holder more than 4 times, and in every draw some list names one holder exactly 4 times.
All inputs are finite; a program needn't handle non-finite values.
Results may differ from the reference program's by a relative error of at most 0.0003.
Values sent between devices are 32-bit elements; how exact they have to be, the bound alone decides.
A program may use at most 64 MiB of HBM per device.

```python
import math
import jax
import jax.numpy as jnp
import numpy as np
from jax import lax

N = 1024
R_DEV = 2048
SPO = 128
ROWS = 131072
SAMPLES = 8192
CAP = 4
N_ROW = 64


def draw_slab_rows(key, part):
    key = jax.random.fold_in(key, 11)
    key_rows, key_cols, key_base = jax.random.split(key, 3)
    row_scale = jnp.exp(jax.random.uniform(key_rows, (ROWS, 1), jnp.float32, math.log(0.3), math.log(3.0)))
    col_scale = jnp.exp(jax.random.uniform(key_cols, (1, N), jnp.float32, math.log(0.3), math.log(3.0)))
    base = jnp.clip(jax.random.normal(key_base, (ROWS, N), jnp.float32), -5.0, 5.0)
    return (base * row_scale * col_scale).astype(jnp.float32)


def set_ends(values, rng, least, largest):
    longest = values.shape.index(max(values.shape))
    spots = []
    for shift in (0, 1):
        where = [jax.random.randint(jax.random.fold_in(rng, axis), (), 0, length) for axis, length in enumerate(values.shape)]
        where[longest] = (where[longest] + shift) % values.shape[longest]
        spots.append(tuple(where))
    return values.at[spots[0]].set(least).at[spots[1]].set(largest)


def deal_out(key, own, number, rows, number_of, top, most, slope):
    order = jax.random.permutation(key, number_of)
    packed, common = load_shares(number_of, rows * top, most, slope, True), load_shares(number_of, rows * top, most, slope, False)
    places = jnp.arange(number_of)

    def named(tallies, offset_by):
        used = int((tallies > 0).sum())
        fixed = max(1, used // 4)
        passed = fixed + (places - fixed + offset_by * (used - fixed)) % max(1, number_of - fixed)
        return jnp.zeros((number_of,), jnp.int32).at[order[jnp.where(places < fixed, places, passed)]].set(jnp.asarray(tallies, jnp.int32))

    tallies = jnp.where(number % 4 == 0, named(packed, number // 4), named(common, number - number // 4 - 1))
    mixed = jax.random.permutation(jax.random.fold_in(own, 3), number_of)
    donor, receiver = mixed[0:number_of // 2 * 2:2], mixed[1:number_of // 2 * 2:2]
    slack = jnp.minimum(tallies[donor] - 1, most - tallies[receiver]) // 2
    slack = jnp.where((donor == order[0]) | (receiver == order[0]) | (tallies[receiver] == 0), 0, jnp.maximum(slack, 0))
    passed = jax.random.randint(jax.random.fold_in(own, 4), (number_of // 2,), 0, 1 << 20) % (slack + 1)
    tallies = tallies.at[donor].add(-passed).at[receiver].add(passed)
    items = jnp.searchsorted(jnp.cumsum(tallies), jnp.arange(rows * top), side="right").astype(jnp.int32)
    grid = items.reshape(top, rows).T
    grid = grid[jax.random.permutation(jax.random.fold_in(own, 1), rows)]
    offset_by = jax.random.randint(jax.random.fold_in(own, 2), (rows, 1), 0, top)
    return jnp.take_along_axis(grid, (jnp.arange(top)[None, :] + offset_by) % top, axis=1)


def load_shares(count, total, limit, lean, full):
    portions = [(1 << 20) // math.isqrt(grade ** lean) + 1 for grade in range(1, count + 1)]
    largest = limit if full else min(limit, max(-(-total // count), total * portions[0] // sum(portions)))
    least = 1 if total - largest >= count - 1 else 0
    holding, rest = [largest] + [least] * (count - 1), total - largest - least * (count - 1)
    while rest > 0:
        free = [i for i in range(1, count) if holding[i] < largest] or [i for i in range(1, count) if holding[i] < limit]
        mass, budget = sum([portions[i] for i in free]), rest
        for i in free:
            extra = min(limit - holding[i], max(1, budget * portions[i] // mass), rest)
            holding[i] = holding[i] + extra
            rest = rest - extra
    return np.array(holding)


def setup_inputs(seed: int = 0) -> dict:
    key_list = jax.random.split(jax.random.key(seed), 5)
    slab_rows = draw_slab_rows(jax.random.fold_in(key_list[4], 71), 0)
    row_flips = set_ends(jax.random.randint(key_list[1], (ROWS,), 0, 2), jax.random.fold_in(key_list[1], 1), 0, 1).astype(jnp.int32)
    sample_holder_keys = jax.random.split(jax.random.fold_in(key_list[2], 1), SAMPLES // SPO)
    sample_holder_turns = jax.random.permutation(jax.random.fold_in(key_list[2], 3), SAMPLES // SPO)
    sample_holder = jax.vmap(lambda own, number: deal_out(jax.random.fold_in(key_list[2], 2), own, number, SPO, N_ROW, 1, CAP, 2))(sample_holder_keys, sample_holder_turns).reshape((SAMPLES, 1))
    sample_offset = set_ends(jax.random.randint(key_list[3], (SAMPLES,), 0, R_DEV), jax.random.fold_in(key_list[3], 1), 0, R_DEV - 1).astype(jnp.int32)
    return {"slab_rows": slab_rows, "row_flips": row_flips, "sample_holder": sample_holder, "sample_offset": sample_offset}


def hadamard(table_size):
    indices = jnp.arange(table_size, dtype=jnp.int32)
    shared = indices[:, None] & indices[None, :]
    parity = jnp.zeros((table_size, table_size), jnp.int32)
    for bit_pos in range(max(table_size.bit_length() - 1, 0)):
        parity = parity ^ shared >> bit_pos & 1
    return (1 - 2 * parity).astype(jnp.float32)

def reference(slab_rows, row_flips, sample_holder, sample_offset):
    total_rows = slab_rows.shape[0]
    columns = slab_rows.shape[1]
    inner = min(R_DEV, 128)
    outer = R_DEV // inner
    signs = (1 - 2 * row_flips).astype(jnp.float32)
    signed = slab_rows * signs[:, None]
    blocks = signed.reshape(N_ROW, outer, inner, columns)
    blocks = jnp.einsum('pb,dabc->dapc', hadamard(inner), blocks, precision=lax.Precision.HIGHEST)
    blocks = jnp.einsum('qa,dapc->dqpc', hadamard(outer), blocks, precision=lax.Precision.HIGHEST)
    blocks = jnp.einsum('ed,dqpc->eqpc', hadamard(N_ROW), blocks, precision=lax.Precision.HIGHEST)
    mixed_slab = blocks.reshape(total_rows, columns) * (1.0 / math.sqrt(total_rows))
    index = (R_DEV * sample_holder[:, 0] + sample_offset).astype(jnp.int32)
    sampled = jnp.take(mixed_slab, index, axis=0)
    gram = jnp.dot(sampled.T.astype(jnp.float32), sampled.astype(jnp.float32), precision=lax.Precision.HIGHEST, preferred_element_type=jnp.float32)
    lower = jnp.linalg.cholesky(gram * (1.0 / SAMPLES))
    return (mixed_slab, lower.T)
```

```python
import functools
import math

import jax
import jax.numpy as jnp
from jax import lax
from jax.experimental import pallas as pl
from jax.experimental.pallas import tpu as pltpu
from jax.sharding import PartitionSpec as P

MESH = pl.DeviceIdType.MESH
PRECISE = lax.Precision.HIGHEST
F32, BF16 = jnp.float32, jnp.bfloat16
TILE = 128


def split_three(values):
    high = values.astype(BF16)
    rest = values - high.astype(F32)
    middle = rest.astype(BF16)
    return high, middle, (rest - middle.astype(F32)).astype(BF16)


def exact_dot(left, values):
    return sum(jnp.dot(left, part, preferred_element_type=F32) for part in split_three(values))


def butterfly(items):
    items, apart = list(items), 1
    while apart < len(items):
        for i in range(len(items)):
            if not i & apart:
                items[i], items[i + apart] = items[i] + items[i + apart], items[i] - items[i + apart]
        apart *= 2
    return items


def wait_for(ref, sem):
    pltpu.make_async_copy(ref, ref, sem).wait()


def mix_kernel(nx, nz, scale, x_ref, sign_ref, key_ref, out_ref, keys_ref, work, recv, back, send_sem, recv_sem):
    n = nx * nz
    blocks, chunk = sign_ref.shape[0], work.shape[1]
    per_block = TILE // chunk
    me, col = lax.axis_index("row"), lax.axis_index("col")
    mx, mz = lax.div(me, nz), lax.rem(me, nz)

    def peer(k):
        dx, m = lax.rem(k, nx), lax.div(k, nx)
        dz = nz + lax.div(m + 1, 2) * (2 * lax.rem(m, 2) - 1)
        return lax.rem(mx + dx, nx) * nz + lax.rem(mz + dz, nz)

    barrier = pltpu.get_barrier_semaphore()

    def greet(k, carry):
        pl.semaphore_signal(barrier, inc=1, device_id=(peer(k), col), device_id_type=MESH)
        return carry

    lax.fori_loop(1, n, greet, 0)

    shared = lax.broadcasted_iota(jnp.int32, (TILE, TILE), 0) & lax.broadcasted_iota(jnp.int32, (TILE, TILE), 1)
    shared = shared ^ shared >> 4
    shared = shared ^ shared >> 2
    shared = shared ^ shared >> 1
    table = (1 - 2 * (shared & 1)).astype(F32)

    def inner(a, carry):
        left = (table * sign_ref[pl.ds(a, 1), :]).astype(BF16)
        rows = x_ref[pl.ds(pl.multiple_of(a * TILE, TILE), TILE), :]
        work[pl.ds(a * per_block, per_block)] = exact_dot(left, rows).reshape(per_block, chunk, TILE)
        return carry

    lax.fori_loop(0, blocks, inner, 0)

    def outer(b, carry):
        part, at = lax.div(b * 8, chunk), pl.multiple_of(lax.rem(b * 8, chunk), 8)
        mixed = butterfly([work[a * per_block + part, pl.ds(at, 8), :] for a in range(blocks)])
        for a in range(blocks):
            work[a * per_block + part, pl.ds(at, 8), :] = mixed[a]
        return carry

    lax.fori_loop(0, TILE // 8, outer, 0)
    pl.semaphore_wait(barrier, n - 1)

    def send(src, dst, device, which):
        pltpu.make_async_remote_copy(
            src_ref=src, dst_ref=dst, send_sem=send_sem.at[which], recv_sem=recv_sem.at[which],
            device_id=(device, col), device_id_type=MESH,
        ).start()

    def there(k, carry):
        device = peer(k)
        send(key_ref, keys_ref.at[me], device, 0)
        send(work.at[device], recv.at[me], device, 1)
        return carry

    lax.fori_loop(1, n, there, 0)
    keys_ref[me] = key_ref[...]
    recv[me] = work[me]
    wait_for(recv.at[pl.ds(0, n - 1)], recv_sem.at[1])

    def low(g, carry):
        mixed = butterfly([recv[8 * g + i] for i in range(8)])
        for i in range(8):
            recv[8 * g + i] = mixed[i]
        return carry

    def high(i, carry):
        mixed = butterfly([recv[8 * g + i] for g in range(n // 8)])
        for g in range(n // 8):
            back[8 * g + i] = mixed[g] * scale
        return carry

    lax.fori_loop(0, n // 8, low, 0)
    lax.fori_loop(0, 8, high, 0)

    def home(k, carry):
        device = peer(k)
        send(back.at[device], out_ref.at[me], device, 2)
        return carry

    lax.fori_loop(1, n, home, 0)
    out_ref[me] = back[me]
    wait_for(keys_ref.at[pl.ds(0, n - 1)], recv_sem.at[0])
    wait_for(out_ref.at[pl.ds(0, n - 1)], recv_sem.at[2])
    wait_for(keys_ref.at[pl.ds(0, n - 1)], send_sem.at[0])
    wait_for(recv.at[pl.ds(0, n - 1)], send_sem.at[1])
    wait_for(out_ref.at[pl.ds(0, n - 1)], send_sem.at[2])


def gram_kernel(nx, nz, nc, local, mixed_ref, keys_ref, gram_ref, packed, part, arrived, middle, pieces, send_sem, recv_sem):
    n, owners = nx * nz, keys_ref.shape[0]
    slots = packed.shape[1]
    capacity = slots // owners
    samples = owners * keys_ref.shape[1]
    rows_x = part.shape[2]
    me, mc = lax.axis_index("row"), lax.axis_index("col")
    mx, mz = lax.div(me, nz), lax.rem(me, nz)

    def along_col(d):
        return me, lax.rem(mc + d, nc)

    def along_x(d):
        return lax.rem(mx + d, nx) * nz + mz, mc

    def along_z(d):
        return mx * nz + lax.rem(mz + d, nz), mc

    barrier = pltpu.get_barrier_semaphore()
    for count, peer in ((nc, along_col), (nx, along_x), (nz, along_z)):
        for d in range(1, count):
            pl.semaphore_signal(barrier, inc=1, device_id=peer(d), device_id_type=MESH)

    holder, offset = keys_ref[...] // local, keys_ref[...] % local
    mine = jnp.where(holder == me, 1.0, 0.0)
    before = lax.broadcasted_iota(jnp.int32, (TILE, TILE), 0) < lax.broadcasted_iota(jnp.int32, (TILE, TILE), 1)
    rank = jnp.dot(mine.astype(BF16), jnp.where(before, 1.0, 0.0).astype(BF16), preferred_element_type=F32)
    wanted = []
    for q in range(capacity):
        chosen = jnp.where(rank == q, mine, 0.0)
        row = jnp.sum(chosen * (offset + 1).astype(F32), axis=1, keepdims=True) - 1.0
        wanted.append(jnp.broadcast_to(row, (owners, TILE)))
    wanted = jnp.concatenate(wanted, axis=0).astype(jnp.int32)
    lanes = lax.broadcasted_iota(jnp.int32, (slots, TILE), 1)

    def pick(a, total):
        chosen = jnp.where(wanted == lanes + a * TILE, 1.0, 0.0).astype(BF16)
        return total + exact_dot(chosen, mixed_ref[pl.ds(pl.multiple_of(a * TILE, TILE), TILE), :])

    packed[mc] = lax.fori_loop(0, local // TILE, pick, jnp.zeros((slots, TILE), F32))
    pl.semaphore_wait(barrier, nc + nx + nz - 3)

    def send(src, dst, device, which):
        pltpu.make_async_remote_copy(
            src_ref=src, dst_ref=dst, send_sem=send_sem.at[which], recv_sem=recv_sem.at[which],
            device_id=device, device_id_type=MESH,
        ).start()

    for d in range(1, nc):
        send(packed.at[mc], packed.at[mc], along_col(d), 0)
    wait_for(packed.at[pl.ds(0, nc - 1)], recv_sem.at[0])
    mine_packed = packed[mc]

    def multiply(b, carry):
        block = lax.dot_general(packed[b], mine_packed, (((0,), (0,)), ((), ())), precision=PRECISE, preferred_element_type=F32)
        for q in range(nx):
            part[q, b] = block[q * rows_x:(q + 1) * rows_x]
        return carry

    lax.fori_loop(0, nc, multiply, 0)
    for d in range(1, nx):
        send(part.at[lax.rem(mx + d, nx)], arrived.at[mx], along_x(d), 1)
    arrived[mx] = part[mx]
    wait_for(arrived.at[pl.ds(0, nx - 1)], recv_sem.at[1])
    total = arrived[0]
    for q in range(1, nx):
        total = total + arrived[q]
    middle[...] = total.reshape(middle.shape)
    for d in range(1, nz):
        send(middle.at[lax.rem(mz + d, nz)], pieces.at[mz], along_z(d), 2)
    pieces[mz] = middle[mz]
    wait_for(pieces.at[pl.ds(0, nz - 1)], recv_sem.at[2])
    total = pieces[0]
    for q in range(1, nz):
        total = total + pieces[q]
    gram_ref[mc, mx, mz] = total * (1.0 / samples)

    own = gram_ref.at[mc, mx, mz]
    for d in range(1, nz):
        send(own, own, along_z(d), 3)
    wait_for(gram_ref.at[mc, mx, pl.ds(0, nz - 1)], recv_sem.at[3])
    own = gram_ref.at[mc, mx]
    for d in range(1, nx):
        send(own, own, along_x(d), 4)
    wait_for(gram_ref.at[mc, pl.ds(0, nx - 1)], recv_sem.at[4])
    own = gram_ref.at[mc]
    for d in range(1, nc):
        send(own, own, along_col(d), 5)
    wait_for(gram_ref.at[pl.ds(0, nc - 1)], recv_sem.at[5])

    wait_for(packed.at[pl.ds(0, nc - 1)], send_sem.at[0])
    wait_for(arrived.at[pl.ds(0, nx - 1)], send_sem.at[1])
    wait_for(pieces.at[pl.ds(0, nz - 1)], send_sem.at[2])
    wait_for(gram_ref.at[mc, mx, pl.ds(0, nz - 1)], send_sem.at[3])
    wait_for(gram_ref.at[mc, pl.ds(0, nx - 1)], send_sem.at[4])
    wait_for(gram_ref.at[pl.ds(0, nc - 1)], send_sem.at[5])


def params(number):
    return pltpu.CompilerParams(collective_id=number, has_side_effects=True, vmem_limit_bytes=40 * 2**20)


def per_device(nx, nz, nc, slab_rows, row_flips, sample_holder, sample_offset):
    local, width = slab_rows.shape
    n = nx * nz
    per_owner = sample_offset.shape[0]
    chunk = local // n
    vmem = pl.BlockSpec(memory_space=pltpu.VMEM)
    signs = (1 - 2 * row_flips).astype(F32).reshape(local // TILE, TILE)
    key = (sample_holder[:, 0] * local + sample_offset).reshape(1, per_owner)
    mixed, keys = pl.pallas_call(
        functools.partial(mix_kernel, nx, nz, 1.0 / math.sqrt(local * n)),
        out_shape=(
            jax.ShapeDtypeStruct((n, chunk, width), F32),
            jax.ShapeDtypeStruct((n, 1, per_owner), jnp.int32),
        ),
        in_specs=[vmem] * 3,
        out_specs=(vmem, vmem),
        scratch_shapes=[pltpu.VMEM((n, chunk, width), F32)] * 3
        + [pltpu.SemaphoreType.DMA((3,)), pltpu.SemaphoreType.DMA((3,))],
        compiler_params=params(0),
        name="mix",
    )(slab_rows, signs, key)
    mixed_slab = mixed.reshape(local, width)
    capacity = 2 * per_owner // n
    rows_x, rows_z = TILE // nx, TILE * nc // (nx * nz)
    gram = pl.pallas_call(
        functools.partial(gram_kernel, nx, nz, nc, local),
        out_shape=jax.ShapeDtypeStruct((nc, nx, nz, rows_z, TILE), F32),
        in_specs=[vmem] * 2,
        out_specs=vmem,
        scratch_shapes=[
            pltpu.VMEM((nc, n * capacity, width), F32),
            pltpu.VMEM((nx, nc, rows_x, TILE), F32),
            pltpu.VMEM((nx, nc, rows_x, TILE), F32),
            pltpu.VMEM((nz, rows_z, TILE), F32),
            pltpu.VMEM((nz, rows_z, TILE), F32),
            pltpu.SemaphoreType.DMA((6,)),
            pltpu.SemaphoreType.DMA((6,)),
        ],
        compiler_params=params(1),
        name="gram",
    )(mixed_slab, keys.reshape(n, per_owner))
    gram = gram.reshape(nc, nx, nc, nz // nc, rows_z, TILE).transpose(2, 1, 3, 4, 0, 5).reshape(nc * TILE, nc * TILE)
    upper = jnp.linalg.cholesky(gram).T
    precond = lax.dynamic_slice_in_dim(upper, lax.axis_index("col") * width, width, 1)
    return (mixed_slab, precond)


def solution(mesh):
    nx = 4
    nz = mesh.shape["row"] // nx
    in_specs = (P("row", "col"), P("row"), P("row", None), P("row"))
    out_specs = (P("row", "col"), P(None, "col"))
    return jax.shard_map(
        functools.partial(per_device, nx, nz, mesh.shape["col"]),
        mesh=mesh, in_specs=in_specs, out_specs=out_specs, check_vma=False,
    )
```

```python
import functools
import math

import jax
import jax.numpy as jnp
from jax import lax
from jax.experimental import pallas as pl
from jax.experimental.pallas import tpu as pltpu
from jax.sharding import PartitionSpec as P

MESH = pl.DeviceIdType.MESH
PRECISE = lax.Precision.HIGHEST
F32, BF16 = jnp.float32, jnp.bfloat16
TILE = 128


def split_three(values):
    high = values.astype(BF16)
    rest = values - high.astype(F32)
    middle = rest.astype(BF16)
    return high, middle, (rest - middle.astype(F32)).astype(BF16)


def exact_dot(left, values):
    return sum(jnp.dot(left, part, preferred_element_type=F32) for part in split_three(values))


def butterfly(items):
    items, apart = list(items), 1
    while apart < len(items):
        for i in range(len(items)):
            if not i & apart:
                items[i], items[i + apart] = items[i] + items[i + apart], items[i] - items[i + apart]
        apart *= 2
    return items


def wait_for(ref, sem):
    pltpu.make_async_copy(ref, ref, sem).wait()


def mix_kernel(nx, nz, scale, x_ref, sign_ref, key_ref, out_ref, keys_ref, work, recv, back, send_sem, recv_sem):
    n = nx * nz
    blocks, chunk = sign_ref.shape[0], work.shape[1]
    per_block = TILE // chunk
    me, col = lax.axis_index("row"), lax.axis_index("col")
    mx, mz = lax.div(me, nz), lax.rem(me, nz)

    def peer(k):
        dx, m = lax.rem(k, nx), lax.div(k, nx)
        dz = nz + lax.div(m + 1, 2) * (2 * lax.rem(m, 2) - 1)
        return lax.rem(mx + dx, nx) * nz + lax.rem(mz + dz, nz)

    barrier = pltpu.get_barrier_semaphore()

    def greet(k, carry):
        pl.semaphore_signal(barrier, inc=1, device_id=(peer(k), col), device_id_type=MESH)
        return carry

    lax.fori_loop(1, n, greet, 0)

    shared = lax.broadcasted_iota(jnp.int32, (TILE, TILE), 0) & lax.broadcasted_iota(jnp.int32, (TILE, TILE), 1)
    shared = shared ^ shared >> 4
    shared = shared ^ shared >> 2
    shared = shared ^ shared >> 1
    table = (1 - 2 * (shared & 1)).astype(F32)

    def inner(a, carry):
        left = (table * sign_ref[pl.ds(a, 1), :]).astype(BF16)
        rows = x_ref[pl.ds(pl.multiple_of(a * TILE, TILE), TILE), :]
        work[pl.ds(a * per_block, per_block)] = exact_dot(left, rows).reshape(per_block, chunk, TILE)
        return carry

    lax.fori_loop(0, blocks, inner, 0)

    def outer(b, carry):
        part, at = lax.div(b * 8, chunk), pl.multiple_of(lax.rem(b * 8, chunk), 8)
        mixed = butterfly([work[a * per_block + part, pl.ds(at, 8), :] for a in range(blocks)])
        for a in range(blocks):
            work[a * per_block + part, pl.ds(at, 8), :] = mixed[a]
        return carry

    lax.fori_loop(0, TILE // 8, outer, 0)
    pl.semaphore_wait(barrier, n - 1)

    def send(src, dst, device, which):
        pltpu.make_async_remote_copy(
            src_ref=src, dst_ref=dst, send_sem=send_sem.at[which], recv_sem=recv_sem.at[which],
            device_id=(device, col), device_id_type=MESH,
        ).start()

    def there(k, carry):
        device = peer(k)
        send(key_ref, keys_ref.at[me], device, 0)
        send(work.at[device], recv.at[me], device, 1)
        return carry

    lax.fori_loop(1, n, there, 0)
    keys_ref[me] = key_ref[...]
    recv[me] = work[me]
    wait_for(recv.at[pl.ds(0, n - 1)], recv_sem.at[1])

    def low(g, carry):
        mixed = butterfly([recv[8 * g + i] for i in range(8)])
        for i in range(8):
            recv[8 * g + i] = mixed[i]
        return carry

    def high(i, carry):
        mixed = butterfly([recv[8 * g + i] for g in range(n // 8)])
        for g in range(n // 8):
            back[8 * g + i] = mixed[g] * scale
        return carry

    lax.fori_loop(0, n // 8, low, 0)
    lax.fori_loop(0, 8, high, 0)

    def home(k, carry):
        device = peer(k)
        send(back.at[device], out_ref.at[me], device, 2)
        return carry

    lax.fori_loop(1, n, home, 0)
    out_ref[me] = back[me]
    wait_for(keys_ref.at[pl.ds(0, n - 1)], recv_sem.at[0])
    wait_for(out_ref.at[pl.ds(0, n - 1)], recv_sem.at[2])
    wait_for(keys_ref.at[pl.ds(0, n - 1)], send_sem.at[0])
    wait_for(recv.at[pl.ds(0, n - 1)], send_sem.at[1])
    wait_for(out_ref.at[pl.ds(0, n - 1)], send_sem.at[2])


def gram_kernel(nx, nz, nc, local, mixed_ref, keys_ref, gram_ref, packed, part, arrived, middle, pieces, send_sem, recv_sem):
    n, owners = nx * nz, keys_ref.shape[0]
    slots = packed.shape[1]
    capacity = slots // owners
    samples = owners * keys_ref.shape[1]
    rows_x = part.shape[2]
    me, mc = lax.axis_index("row"), lax.axis_index("col")
    mx, mz = lax.div(me, nz), lax.rem(me, nz)

    def along_col(d):
        return me, lax.rem(mc + d, nc)

    def along_x(d):
        return lax.rem(mx + d, nx) * nz + mz, mc

    def along_z(d):
        return mx * nz + lax.rem(mz + d, nz), mc

    barrier = pltpu.get_barrier_semaphore()
    for count, peer in ((nc, along_col), (nx, along_x), (nz, along_z)):
        for d in range(1, count):
            pl.semaphore_signal(barrier, inc=1, device_id=peer(d), device_id_type=MESH)

    holder, offset = keys_ref[...] // local, keys_ref[...] % local
    mine = jnp.where(holder == me, 1.0, 0.0)
    before = lax.broadcasted_iota(jnp.int32, (TILE, TILE), 0) < lax.broadcasted_iota(jnp.int32, (TILE, TILE), 1)
    rank = jnp.dot(mine.astype(BF16), jnp.where(before, 1.0, 0.0).astype(BF16), preferred_element_type=F32)
    wanted = []
    for q in range(capacity):
        chosen = jnp.where(rank == q, mine, 0.0)
        row = jnp.sum(chosen * (offset + 1).astype(F32), axis=1, keepdims=True) - 1.0
        wanted.append(jnp.broadcast_to(row, (owners, TILE)))
    wanted = jnp.concatenate(wanted, axis=0).astype(jnp.int32)
    lanes = lax.broadcasted_iota(jnp.int32, (slots, TILE), 1)

    def pick(a, total):
        chosen = jnp.where(wanted == lanes + a * TILE, 1.0, 0.0).astype(BF16)
        return total + exact_dot(chosen, mixed_ref[pl.ds(pl.multiple_of(a * TILE, TILE), TILE), :])

    packed[mc] = lax.fori_loop(0, local // TILE, pick, jnp.zeros((slots, TILE), F32))
    pl.semaphore_wait(barrier, nc + nx + nz - 3)

    def send(src, dst, device, which):
        pltpu.make_async_remote_copy(
            src_ref=src, dst_ref=dst, send_sem=send_sem.at[which], recv_sem=recv_sem.at[which],
            device_id=device, device_id_type=MESH,
        ).start()

    for d in range(1, nc):
        send(packed.at[mc], packed.at[mc], along_col(d), 0)
    wait_for(packed.at[pl.ds(0, nc - 1)], recv_sem.at[0])
    mine_packed = packed[mc]

    def multiply(b, carry):
        block = lax.dot_general(packed[b], mine_packed, (((0,), (0,)), ((), ())), precision=PRECISE, preferred_element_type=F32)
        for q in range(nx):
            part[q, b] = block[q * rows_x:(q + 1) * rows_x]
        return carry

    lax.fori_loop(0, nc, multiply, 0)
    for d in range(1, nx):
        send(part.at[lax.rem(mx + d, nx)], arrived.at[mx], along_x(d), 1)
    arrived[mx] = part[mx]
    wait_for(arrived.at[pl.ds(0, nx - 1)], recv_sem.at[1])
    total = arrived[0]
    for q in range(1, nx):
        total = total + arrived[q]
    middle[...] = total.reshape(middle.shape)
    for d in range(1, nz):
        send(middle.at[lax.rem(mz + d, nz)], pieces.at[mz], along_z(d), 2)
    pieces[mz] = middle[mz]
    wait_for(pieces.at[pl.ds(0, nz - 1)], recv_sem.at[2])
    total = pieces[0]
    for q in range(1, nz):
        total = total + pieces[q]
    gram_ref[mc, mx, mz] = total * (1.0 / samples)

    own = gram_ref.at[mc, mx, mz]
    for d in range(1, nz):
        send(own, own, along_z(d), 3)
    wait_for(gram_ref.at[mc, mx, pl.ds(0, nz - 1)], recv_sem.at[3])
    own = gram_ref.at[mc, mx]
    for d in range(1, nx):
        send(own, own, along_x(d), 4)
    wait_for(gram_ref.at[mc, pl.ds(0, nx - 1)], recv_sem.at[4])
    own = gram_ref.at[mc]
    for d in range(1, nc):
        send(own, own, along_col(d), 5)
    wait_for(gram_ref.at[pl.ds(0, nc - 1)], recv_sem.at[5])

    wait_for(packed.at[pl.ds(0, nc - 1)], send_sem.at[0])
    wait_for(arrived.at[pl.ds(0, nx - 1)], send_sem.at[1])
    wait_for(pieces.at[pl.ds(0, nz - 1)], send_sem.at[2])
    wait_for(gram_ref.at[mc, mx, pl.ds(0, nz - 1)], send_sem.at[3])
    wait_for(gram_ref.at[mc, pl.ds(0, nx - 1)], send_sem.at[4])
    wait_for(gram_ref.at[pl.ds(0, nc - 1)], send_sem.at[5])


def left_parts(values):
    high, middle, low = split_three(values)
    return jnp.concatenate([high, high, middle, middle, high, low], axis=1)

def right_parts(values):
    high, middle, low = split_three(values)
    return jnp.concatenate([high, middle, high, middle, low, high], axis=0)

def over_rows(row):
    return jnp.broadcast_to(row, (8, TILE))

def inverse(p):
    r = pl.reciprocal(p, approx=True)
    return r * (2.0 - p * r)

def factor(block):
    groups = TILE // 8
    sub = lax.broadcasted_iota(jnp.int32, (8, TILE), 0)
    lane = lax.broadcasted_iota(jnp.int32, (8, TILE), 1)
    s = [block[8 * g:8 * g + 8] for g in range(groups)]
    e = [jnp.where(sub + 8 * g == lane, 1.0, 0.0) for g in range(groups)]
    for t in range(groups):
        cols = [{g: jnp.broadcast_to(s[g][:, 8 * t + j:8 * t + j + 1], (8, TILE)) for g in range(t, groups)} for j in range(8)]
        pivots = jnp.zeros((8, TILE), F32)
        for j in range(8):
            pivot = over_rows(cols[j][t][j:j + 1])
            pivots = jnp.where(sub == j, pivot, pivots)
            r = inverse(pivot)
            heads = {l: over_rows(cols[l][t][j:j + 1]) for l in range(j + 1, 8)}
            head_s, head_e = over_rows(s[t][j:j + 1]), over_rows(e[t][j:j + 1])
            for g in range(t, groups):
                m = cols[j][g] * r
                if g == t:
                    m = jnp.where(sub > j, m, 0.0)
                for l in range(j + 1, 8):
                    cols[l][g] = cols[l][g] - m * heads[l]
                s[g] = s[g] - m * head_s
                e[g] = e[g] - m * head_e
        root = lax.rsqrt(pivots)
        s[t] = jnp.where(lane >= sub + 8 * t, s[t] * root, 0.0)
        e[t] = e[t] * root
    return jnp.concatenate(s, axis=0), jnp.concatenate(e, axis=0)

def chol_kernel(nc, load, mc, gram_ref, out_ref, work, row, right):
    def fill(c, carry):
        for k in range(nc):
            work[k, :, pl.ds(pl.multiple_of(c * TILE, TILE), TILE)] = load(gram_ref, k, c)
        return carry
    lax.fori_loop(0, nc, fill, 0)

    def step(k, carry):
        own = pl.ds(pl.multiple_of(k * TILE, TILE), TILE)
        upper, inv = factor(work[k, :, own])
        left = left_parts(inv)
        def panel(j, carry):
            at = pl.ds(pl.multiple_of(j * TILE, TILE), TILE)
            got = jnp.dot(left, right_parts(work[k, :, at]), preferred_element_type=F32)
            row[:, at] = got
            right[:, at] = right_parts(got)
            return carry
        lax.fori_loop(k + 1, nc, panel, 0)
        row[:, own] = upper
        mine = row[:, pl.ds(pl.multiple_of(mc * TILE, TILE), TILE)]
        out_ref[pl.ds(pl.multiple_of(k * TILE, TILE), TILE), :] = jnp.where(mc >= k, mine, 0.0)
        def trail(i, carry):
            at = pl.ds(pl.multiple_of(i * TILE, TILE), TILE)
            turned = left_parts(row[:, at].T)
            work[i] = work[i] - jnp.dot(turned, right[...], preferred_element_type=F32)
            return carry
        lax.fori_loop(k + 1, nc, trail, 0)
        return carry
    lax.fori_loop(0, nc, step, 0)


def params(number):
    return pltpu.CompilerParams(collective_id=number, has_side_effects=True, vmem_limit_bytes=40 * 2**20)


def per_device(nx, nz, nc, slab_rows, row_flips, sample_holder, sample_offset):
    local, width = slab_rows.shape
    n = nx * nz
    per_owner = sample_offset.shape[0]
    chunk = local // n
    vmem = pl.BlockSpec(memory_space=pltpu.VMEM)
    signs = (1 - 2 * row_flips).astype(F32).reshape(local // TILE, TILE)
    key = (sample_holder[:, 0] * local + sample_offset).reshape(1, per_owner)
    mixed, keys = pl.pallas_call(
        functools.partial(mix_kernel, nx, nz, 1.0 / math.sqrt(local * n)),
        out_shape=(
            jax.ShapeDtypeStruct((n, chunk, width), F32),
            jax.ShapeDtypeStruct((n, 1, per_owner), jnp.int32),
        ),
        in_specs=[vmem] * 3,
        out_specs=(vmem, vmem),
        scratch_shapes=[pltpu.VMEM((n, chunk, width), F32)] * 3
        + [pltpu.SemaphoreType.DMA((3,)), pltpu.SemaphoreType.DMA((3,))],
        compiler_params=params(0),
        name="mix",
    )(slab_rows, signs, key)
    mixed_slab = mixed.reshape(local, width)
    capacity = 2 * per_owner // n
    rows_x, rows_z = TILE // nx, TILE * nc // (nx * nz)
    gram = pl.pallas_call(
        functools.partial(gram_kernel, nx, nz, nc, local),
        out_shape=jax.ShapeDtypeStruct((nc, nx, nz, rows_z, TILE), F32),
        in_specs=[vmem] * 2,
        out_specs=vmem,
        scratch_shapes=[
            pltpu.VMEM((nc, n * capacity, width), F32),
            pltpu.VMEM((nx, nc, rows_x, TILE), F32),
            pltpu.VMEM((nx, nc, rows_x, TILE), F32),
            pltpu.VMEM((nz, rows_z, TILE), F32),
            pltpu.VMEM((nz, rows_z, TILE), F32),
            pltpu.SemaphoreType.DMA((6,)),
            pltpu.SemaphoreType.DMA((6,)),
        ],
        compiler_params=params(1),
        name="gram",
    )(mixed_slab, keys.reshape(n, per_owner))
    per_block = nz // nc

    def block(ref, k, c):
        return ref[c, :, per_block * k:per_block * (k + 1)].reshape(TILE, TILE)

    def root_kernel(gram_ref, out_ref, *scratch):
        chol_kernel(nc, block, lax.axis_index("col"), gram_ref, out_ref, *scratch)

    precond = pl.pallas_call(
        root_kernel,
        out_shape=jax.ShapeDtypeStruct((nc * TILE, width), F32),
        in_specs=[vmem],
        out_specs=vmem,
        scratch_shapes=[
            pltpu.VMEM((nc, TILE, nc * TILE), F32),
            pltpu.VMEM((TILE, nc * TILE), F32),
            pltpu.VMEM((6 * TILE, nc * TILE), BF16),
        ],
        compiler_params=pltpu.CompilerParams(vmem_limit_bytes=40 * 2**20),
        name="root",
    )(gram)
    return (mixed_slab, precond)


def solution(mesh):
    nx = 4
    nz = mesh.shape["row"] // nx
    in_specs = (P("row", "col"), P("row"), P("row", None), P("row"))
    out_specs = (P("row", "col"), P(None, "col"))
    return jax.shard_map(
        functools.partial(per_device, nx, nz, mesh.shape["col"]),
        mesh=mesh, in_specs=in_specs, out_specs=out_specs, check_vma=False,
    )
```

```python
import functools
import math

import jax
import jax.numpy as jnp
from jax import lax
from jax.experimental import pallas as pl
from jax.experimental.pallas import tpu as pltpu
from jax.sharding import PartitionSpec as P

MESH = pl.DeviceIdType.MESH
F32, BF16 = jnp.float32, jnp.bfloat16
TILE = 128


def split_three(values):
    high = values.astype(BF16)
    rest = values - high.astype(F32)
    middle = rest.astype(BF16)
    return high, middle, (rest - middle.astype(F32)).astype(BF16)


def exact_dot(left, values):
    return sum(jnp.dot(left, part, preferred_element_type=F32) for part in split_three(values))


def butterfly(items):
    items, apart = list(items), 1
    while apart < len(items):
        for i in range(len(items)):
            if not i & apart:
                items[i], items[i + apart] = items[i] + items[i + apart], items[i] - items[i + apart]
        apart *= 2
    return items


def wait_for(ref, sem):
    pltpu.make_async_copy(ref, ref, sem).wait()


def left_parts(values):
    high, middle, low = split_three(values)
    return jnp.concatenate([high, high, middle, middle, high, low], axis=1)


def right_parts(values):
    high, middle, low = split_three(values)
    return jnp.concatenate([high, middle, high, middle, low, high], axis=0)


def over_rows(row):
    return jnp.broadcast_to(row, (8, TILE))


def inverse(p):
    r = pl.reciprocal(p, approx=True)
    return r * (2.0 - p * r)


def factor(block):
    groups = TILE // 8
    sub = lax.broadcasted_iota(jnp.int32, (8, TILE), 0)
    lane = lax.broadcasted_iota(jnp.int32, (8, TILE), 1)
    s = [block[8 * g:8 * g + 8] for g in range(groups)]
    e = [jnp.where(sub + 8 * g == lane, 1.0, 0.0) for g in range(groups)]
    for t in range(groups):
        cols = [{g: jnp.broadcast_to(s[g][:, 8 * t + j:8 * t + j + 1], (8, TILE)) for g in range(t, groups)} for j in range(8)]
        pivots = jnp.zeros((8, TILE), F32)
        for j in range(8):
            pivot = over_rows(cols[j][t][j:j + 1])
            pivots = jnp.where(sub == j, pivot, pivots)
            r = inverse(pivot)
            heads = {l: over_rows(cols[l][t][j:j + 1]) for l in range(j + 1, 8)}
            head_s, head_e = over_rows(s[t][j:j + 1]), over_rows(e[t][j:j + 1])
            for g in range(t, groups):
                m = cols[j][g] * r
                if g == t:
                    m = jnp.where(sub > j, m, 0.0)
                for l in range(j + 1, 8):
                    cols[l][g] = cols[l][g] - m * heads[l]
                s[g] = s[g] - m * head_s
                e[g] = e[g] - m * head_e
        root = lax.rsqrt(pivots)
        s[t] = jnp.where(lane >= sub + 8 * t, s[t] * root, 0.0)
        e[t] = e[t] * root
    return jnp.concatenate(s, axis=0), jnp.concatenate(e, axis=0)


def chol_kernel(nc, load, mc, gram_ref, out_ref, work, row, right):
    for k in range(nc):
        for c in range(k, nc):
            work[k, :, c * TILE:(c + 1) * TILE] = load(gram_ref, k, c)

    def step(k, carry):
        own = pl.ds(pl.multiple_of(k * TILE, TILE), TILE)
        upper, inv = factor(work[k, :, own])
        left = left_parts(inv)
        def panel(j, carry):
            at = pl.ds(pl.multiple_of(j * TILE, TILE), TILE)
            got = jnp.dot(left, right_parts(work[k, :, at]), preferred_element_type=F32)
            row[:, at] = got
            right[:, at] = right_parts(got)
            return carry
        lax.fori_loop(k + 1, nc, panel, 0)
        row[:, own] = upper
        mine = row[:, pl.ds(pl.multiple_of(mc * TILE, TILE), TILE)]
        out_ref[pl.ds(pl.multiple_of(k * TILE, TILE), TILE), :] = jnp.where(mc >= k, mine, 0.0)
        def trail(i, carry):
            at = pl.ds(pl.multiple_of(i * TILE, TILE), TILE)
            turned = left_parts(row[:, at].T)
            work[i] = work[i] - jnp.dot(turned, right[...], preferred_element_type=F32)
            return carry
        lax.fori_loop(k + 1, nc, trail, 0)
        return carry
    lax.fori_loop(0, nc, step, 0)


class Plan:
    def __init__(self, nx, nz, nc, local, per_owner):
        self.nx, self.nz, self.nc, self.n, self.ny = nx, nz, nc, nx * nz, nc // 2
        self.local, self.samples = local, per_owner * self.n
        self.chunk = local // self.n
        self.pairs = [(k, c) for k in range(nc) for c in range(k, nc)]
        per_x = -(-len(self.pairs) // nx)
        self.per_z = -(-per_x // nz)
        self.owners = -(-per_x // self.per_z)
        self.per_x = self.per_z * self.owners
        self.blocks = nx * self.per_x
        self.strip = TILE // nc


def mix_kernel(
    plan, x_ref, sign_ref, key_ref, out_ref, gram_ref, keys_ref, work, recv, back, gathered, left, right, parts, from_core,
    from_y, over_y, from_x, from_z, send_sem, recv_sem, y_sem,
):
    nx, nz, n, nc, ny, local = plan.nx, plan.nz, plan.n, plan.nc, plan.ny, plan.local
    scale = 1.0 / math.sqrt(local * n)
    blocks, chunk = sign_ref.shape[0], work.shape[1]
    per_block = TILE // chunk
    me, col = lax.axis_index("row"), lax.axis_index("col")
    mx, mz = lax.div(me, nz), lax.rem(me, nz)
    my, core = lax.div(col, 2), lax.rem(col, 2)
    strip = core * ny + my
    sibling = (me, col + 1 - 2 * core)

    def peer(k):
        dx, m = lax.rem(k, nx), lax.div(k, nx)
        dz = nz + lax.div(m + 1, 2) * (2 * lax.rem(m, 2) - 1)
        return lax.rem(mx + dx, nx) * nz + lax.rem(mz + dz, nz)

    barrier = pltpu.get_barrier_semaphore()

    def greet(k, carry):
        pl.semaphore_signal(barrier, inc=1, device_id=(peer(k), col), device_id_type=MESH)
        return carry

    lax.fori_loop(1, n, greet, 0)
    for d in range(1, nc):
        pl.semaphore_signal(barrier, inc=1, device_id=(me, lax.rem(col + d, nc)), device_id_type=MESH)

    shared = lax.broadcasted_iota(jnp.int32, (TILE, TILE), 0) & lax.broadcasted_iota(jnp.int32, (TILE, TILE), 1)
    shared = shared ^ shared >> 4
    shared = shared ^ shared >> 2
    shared = shared ^ shared >> 1
    table = (1 - 2 * (shared & 1)).astype(F32)

    def inner(a, carry):
        left = (table * sign_ref[pl.ds(a, 1), :]).astype(BF16)
        rows = x_ref[pl.ds(pl.multiple_of(a * TILE, TILE), TILE), :]
        work[pl.ds(a * per_block, per_block)] = exact_dot(left, rows).reshape(per_block, chunk, TILE)
        return carry

    lax.fori_loop(0, blocks, inner, 0)

    def outer(b, carry):
        part, at = lax.div(b * 8, chunk), pl.multiple_of(lax.rem(b * 8, chunk), 8)
        mixed = butterfly([work[a * per_block + part, pl.ds(at, 8), :] for a in range(blocks)])
        for a in range(blocks):
            work[a * per_block + part, pl.ds(at, 8), :] = mixed[a]
        return carry

    lax.fori_loop(0, TILE // 8, outer, 0)
    pl.semaphore_wait(barrier, n + nc - 2)

    def send(src, dst, device, which, arrival=None):
        pltpu.make_async_remote_copy(
            src_ref=src, dst_ref=dst, send_sem=send_sem.at[which],
            recv_sem=recv_sem.at[which] if arrival is None else arrival,
            device_id=device, device_id_type=MESH,
        ).start()

    def there(k, carry):
        device = (peer(k), col)
        send(key_ref, keys_ref.at[me], device, 0)
        send(work.at[device[0]], recv.at[me], device, 1)
        return carry

    lax.fori_loop(1, n, there, 0)
    keys_ref[me] = key_ref[...]
    recv[me] = work[me]

    per_col = n // nc
    rows = per_col * plan.chunk
    wait_for(keys_ref.at[pl.ds(0, n - 1)], recv_sem.at[0])
    bins = lax.broadcasted_iota(jnp.int32, (rows, TILE), 0)

    def count(o, total):
        key = keys_ref[o]
        holder, offset = key // local - col * per_col, key % local - me * plan.chunk
        here = (holder >= 0) & (holder < per_col) & (offset >= 0) & (offset < plan.chunk)
        where = jnp.where(here, holder * plan.chunk + offset, -1)
        return total + jnp.where(bins == where, 1.0, 0.0)

    counts = jnp.sum(lax.fori_loop(0, n, count, jnp.zeros((rows, TILE), F32)), axis=1, keepdims=True)
    wait_for(recv.at[pl.ds(0, n - 1)], recv_sem.at[1])
    radix = min(8, n)

    def low(g, carry):
        mixed = butterfly([recv[radix * g + i] for i in range(radix)])
        for i in range(radix):
            recv[radix * g + i] = mixed[i]
        return carry

    def high(i, carry):
        mixed = butterfly([recv[radix * g + i] for g in range(n // radix)])
        for g in range(n // radix):
            back[radix * g + i] = mixed[g] * scale
        return carry

    lax.fori_loop(0, n // radix, low, 0)
    lax.fori_loop(0, radix, high, 0)

    for d in range(1, nc):
        to = lax.rem(col + d, nc)
        send(back.at[pl.ds(to * per_col, per_col)], gathered.at[col], (me, to), 3)

    def home(k, carry):
        device = peer(k)
        send(back.at[device], out_ref.at[me], (device, col), 2)
        return carry

    lax.fori_loop(1, n, home, 0)
    out_ref[me] = back[me]
    gathered[col] = back[pl.ds(col * per_col, per_col)]
    wait_for(gathered.at[pl.ds(0, nc - 1)], recv_sem.at[3])

    for c in range(nc):
        here = gathered[c].reshape(rows, TILE)
        right[:, c * TILE:(c + 1) * TILE] = right_parts(here)
        left[c * TILE:(c + 1) * TILE, :] = left_parts((here * counts).T)
    for first in range(0, nc, 2):
        wide = jnp.dot(left[:(first + 2) * TILE, :], right[:, first * TILE:(first + 2) * TILE], preferred_element_type=F32)
        for c in (first, first + 1):
            for k in range(c + 1):
                block = wide[k * TILE:(k + 1) * TILE, (c - first) * TILE:(c - first + 1) * TILE]
                parts[:, plan.pairs.index((k, c))] = block.reshape(nc, plan.strip, TILE)

    send(parts.at[pl.ds((1 - core) * ny, ny)], from_core, sibling, 4)
    wait_for(from_core, recv_sem.at[4])

    def pair(q, carry):
        over_y[q] = parts[core * ny + q] + from_core[q]
        return carry

    lax.fori_loop(0, ny, pair, 0)
    for d in range(1, ny):
        to = lax.rem(my + d, ny)
        send(over_y.at[to], from_y.at[my], (me, to * 2 + core), 5)
    from_y[my] = over_y[my]
    if ny > 1:
        wait_for(from_y.at[pl.ds(0, ny - 1)], recv_sem.at[5])
    own = over_y.at[my]
    total = from_y[0]
    for q in range(1, ny):
        total = total + from_y[q]
    if ny > 1:
        wait_for(over_y.at[pl.ds(0, ny - 1)], send_sem.at[5])
    over_y[my] = total

    def share(q):
        return own.at[pl.ds(q * plan.per_x, plan.per_x)]

    for d in range(1, nx):
        to = lax.rem(mx + d, nx)
        send(share(to), from_x.at[mx], (to * nz + mz, col), 6)
    from_x[mx] = over_y[my, pl.ds(mx * plan.per_x, plan.per_x)]
    wait_for(from_x.at[pl.ds(0, nx - 1)], recv_sem.at[6])
    total = from_x[0]
    for q in range(1, nx):
        total = total + from_x[q]
    wait_for(from_x.at[pl.ds(0, nx - 1)], send_sem.at[6])
    from_x[mx] = total
    slot = plan.per_z

    def piece(ref, q):
        return ref.at[pl.ds(q * slot, slot)]

    for q in range(plan.owners):
        @pl.when(mz != q)
        def _():
            send(piece(from_x.at[mx], q), from_z.at[mz], (mx * nz + q, col), 7)

    @pl.when(mz < plan.owners)
    def _():
        from_z[mz] = from_x[mx, pl.ds(mz * slot, slot)]
        wait_for(from_z.at[pl.ds(0, nz - 1)], recv_sem.at[7])
        total = from_z[0]
        for q in range(1, nz):
            total = total + from_z[q]
        gram_ref[strip, pl.ds(mx * plan.per_x + mz * slot, slot)] = total * (1.0 / plan.samples)
        mine = gram_ref.at[strip, pl.ds(mx * plan.per_x + mz * slot, slot)]
        for d in range(1, nz):
            send(mine, mine, (mx * nz + lax.rem(mz + d, nz), col), 8)
        if plan.owners > 1:
            wait_for(gram_ref.at[strip, pl.ds(0, plan.per_x - slot)], recv_sem.at[8])

    @pl.when(mz >= plan.owners)
    def _():
        other = gram_ref.at[strip, pl.ds(mx * plan.per_x, plan.per_x)]
        wait_for(other, recv_sem.at[8])

    mine = gram_ref.at[strip, pl.ds(mx * plan.per_x, plan.per_x)]
    for d in range(1, nx):
        send(mine, mine, (lax.rem(mx + d, nx) * nz + mz, col), 9)
    wait_for(gram_ref.at[strip, pl.ds(0, plan.blocks - plan.per_x)], recv_sem.at[9])
    mine = gram_ref.at[strip]
    send(mine, mine, sibling, 11)
    for d in range(1, ny):
        send(mine, mine, (me, lax.rem(my + d, ny) * 2 + core), 10, y_sem.at[my])
    for d in range(1, ny):
        q = lax.rem(my + d, ny)
        other = gram_ref.at[core * ny + q]
        wait_for(other, y_sem.at[q])
        send(other, other, sibling, 11)
    wait_for(gram_ref.at[pl.ds(0, ny)], recv_sem.at[11])

    wait_for(out_ref.at[pl.ds(0, n - 1)], recv_sem.at[2])
    wait_for(keys_ref.at[pl.ds(0, n - 1)], send_sem.at[0])
    wait_for(recv.at[pl.ds(0, n - 1)], send_sem.at[1])
    wait_for(out_ref.at[pl.ds(0, n - 1)], send_sem.at[2])
    wait_for(gathered.at[pl.ds(0, nc - 1)], send_sem.at[3])
    wait_for(from_core, send_sem.at[4])
    @pl.when(mz < plan.owners)
    def _():
        if plan.owners > 1:
            wait_for(from_x.at[0, pl.ds(0, (plan.owners - 1) * slot)], send_sem.at[7])
        wait_for(from_z.at[pl.ds(0, nz - 1)], send_sem.at[8])

    @pl.when(mz >= plan.owners)
    def _():
        wait_for(from_x.at[0], send_sem.at[7])

    wait_for(gram_ref.at[strip, pl.ds(0, plan.blocks - plan.per_x)], send_sem.at[9])
    if ny > 1:
        wait_for(gram_ref.at[pl.ds(0, ny - 1)], send_sem.at[10])
    wait_for(gram_ref.at[pl.ds(0, ny)], send_sem.at[11])


def per_device(nx, nz, nc, slab_rows, row_flips, sample_holder, sample_offset):
    local, width = slab_rows.shape
    per_owner = sample_offset.shape[0]
    plan = Plan(nx, nz, nc, local, per_owner)
    n, ny, chunk, strip = plan.n, plan.ny, plan.chunk, plan.strip
    rows = n // nc * chunk
    vmem = pl.BlockSpec(memory_space=pltpu.VMEM)
    signs = (1 - 2 * row_flips).astype(F32).reshape(local // TILE, TILE)
    key = (sample_holder[:, 0] * local + sample_offset).reshape(1, per_owner)

    def buffer(*shape, dtype=F32):
        return pltpu.VMEM(shape, dtype)

    mixed, gram = pl.pallas_call(
        functools.partial(mix_kernel, plan),
        out_shape=(
            jax.ShapeDtypeStruct((n, chunk, width), F32),
            jax.ShapeDtypeStruct((nc, plan.blocks, strip, TILE), F32),
        ),
        in_specs=[vmem] * 3,
        out_specs=(vmem, vmem),
        scratch_shapes=[
            buffer(n, 1, per_owner, dtype=jnp.int32),
            buffer(n, chunk, width),
            buffer(n, chunk, width),
            buffer(n, chunk, width),
            buffer(nc, n // nc, chunk, width),
            buffer(nc * TILE, 6 * rows, dtype=BF16),
            buffer(6 * rows, nc * TILE, dtype=BF16),
            buffer(nc, plan.blocks, strip, TILE),
            buffer(ny, plan.blocks, strip, TILE),
            buffer(ny, plan.blocks, strip, TILE),
            buffer(ny, plan.blocks, strip, TILE),
            buffer(nx, plan.per_x, strip, TILE),
            buffer(nz, plan.per_z, strip, TILE),
            pltpu.SemaphoreType.DMA((12,)),
            pltpu.SemaphoreType.DMA((12,)),
            pltpu.SemaphoreType.DMA((ny,)),
        ],
        compiler_params=pltpu.CompilerParams(collective_id=0, has_side_effects=True, vmem_limit_bytes=48 * 2**20),
        name="mix",
    )(slab_rows, signs, key)

    def block(ref, k, c):
        return ref[:, plan.pairs.index((k, c))].reshape(TILE, TILE)

    def root_kernel(gram_ref, out_ref, *scratch):
        chol_kernel(nc, block, lax.axis_index("col"), gram_ref, out_ref, *scratch)

    precond = pl.pallas_call(
        root_kernel,
        out_shape=jax.ShapeDtypeStruct((nc * TILE, width), F32),
        in_specs=[vmem],
        out_specs=vmem,
        scratch_shapes=[
            buffer(nc, TILE, nc * TILE),
            buffer(TILE, nc * TILE),
            buffer(6 * TILE, nc * TILE, dtype=BF16),
        ],
        compiler_params=pltpu.CompilerParams(vmem_limit_bytes=40 * 2**20),
        name="root",
    )(gram)
    return (mixed.reshape(local, width), precond)


def solution(mesh):
    nx = 4
    nz = mesh.shape["row"] // nx
    in_specs = (P("row", "col"), P("row"), P("row", None), P("row"))
    out_specs = (P("row", "col"), P(None, "col"))
    return jax.shard_map(
        functools.partial(per_device, nx, nz, mesh.shape["col"]),
        mesh=mesh, in_specs=in_specs, out_specs=out_specs, check_vma=False,
    )
```

```python
import functools
import math

import jax
import jax.numpy as jnp
from jax import lax
from jax.experimental import pallas as pl
from jax.experimental.pallas import tpu as pltpu
from jax.sharding import PartitionSpec as P

MESH = pl.DeviceIdType.MESH
F32, BF16 = jnp.float32, jnp.bfloat16
TILE = 128


def split_three(values):
    high = values.astype(BF16)
    rest = values - high.astype(F32)
    middle = rest.astype(BF16)
    return high, middle, (rest - middle.astype(F32)).astype(BF16)


def exact_dot(left, values):
    return sum(jnp.dot(left, part, preferred_element_type=F32) for part in split_three(values))


def butterfly(items):
    items, apart = list(items), 1
    while apart < len(items):
        for i in range(len(items)):
            if not i & apart:
                items[i], items[i + apart] = items[i] + items[i + apart], items[i] - items[i + apart]
        apart *= 2
    return items


def wait_for(ref, sem):
    pltpu.make_async_copy(ref, ref, sem).wait()


def left_parts(values):
    high, middle, low = split_three(values)
    return jnp.concatenate([high, high, middle, middle, high, low], axis=1)


def right_parts(values):
    high, middle, low = split_three(values)
    return jnp.concatenate([high, middle, high, middle, low, high], axis=0)


def factor(block):
    sub = lax.broadcasted_iota(jnp.int32, (8, TILE), 0)
    lane = lax.broadcasted_iota(jnp.int32, (8, TILE), 1)
    row = lax.broadcasted_iota(jnp.int32, (TILE, TILE), 0)
    s, e = block, jnp.where(row == lax.broadcasted_iota(jnp.int32, (TILE, TILE), 1), 1.0, 0.0)
    upper, inverse = [], []
    for t in range(TILE // 8):
        rows = s.shape[0]
        cols = [jnp.broadcast_to(s[:, 8 * t + j:8 * t + j + 1], (rows, TILE)) for j in range(8)]
        pivots = jnp.zeros((8, TILE), F32)
        for j in range(8):
            pivot = jnp.broadcast_to(cols[j][j:j + 1], (8, TILE))
            pivots = jnp.where(sub == j, pivot, pivots)
            r = pl.reciprocal(pivot, approx=True)
            r = r * (2.0 - pivot * r)
            m = jnp.where(row[:rows] > j, cols[j] * r[0:1], 0.0)
            for l in range(j + 1, 8):
                cols[l] = cols[l] - m * cols[l][j:j + 1]
            s, e = s - m * s[j:j + 1], e - m * e[j:j + 1]
        root = lax.rsqrt(pivots)
        upper.append(jnp.where(lane >= sub + 8 * t, s[:8] * root, 0.0))
        inverse.append(e[:8] * root)
        s, e = s[8:], e[8:]
    return jnp.concatenate(upper, axis=0), jnp.concatenate(inverse, axis=0)


def root_of(nc, load, mc, out_ref, table, left, right):
    for k in range(nc):
        for c in range(k, nc):
            table[k * TILE:(k + 1) * TILE, c * TILE:(c + 1) * TILE] = load(k, c)

    def step(i, carry):
        at = pl.ds(pl.multiple_of(i * TILE, TILE), TILE)
        upper, inverse = factor(table[at, at])
        out_ref[at, :] = jnp.where(mc == i, upper, 0.0)
        first = left_parts(inverse)
        for k in range(nc - 1):
            @pl.when(i == k)
            def _():
                end = (k + 1) * TILE
                row = jnp.dot(first, right_parts(table[k * TILE:end, end:]), preferred_element_type=F32)
                right[:6 * TILE, end:] = right_parts(row)
                for c in range(k + 1, nc):
                    block = row[:, (c - k - 1) * TILE:(c - k) * TILE]
                    left[c * TILE:(c + 1) * TILE, :6 * TILE] = left_parts(block.T)

                    @pl.when(mc == c)
                    def _():
                        out_ref[k * TILE:end, :] = block
                for c in range((k + 1) // 2 * 2, nc, 2):
                    cols = slice(max(c, k + 1) * TILE, (c + 2) * TILE)
                    rows = slice(end, (c + 2) * TILE)
                    table[rows, cols] = table[rows, cols] - jnp.dot(
                        left[rows, :6 * TILE], right[:6 * TILE, cols], preferred_element_type=F32
                    )
        return carry

    lax.fori_loop(0, nc, step, 0)


class Plan:
    def __init__(self, nx, nz, nc, local, per_owner):
        self.nx, self.nz, self.nc, self.n, self.ny = nx, nz, nc, nx * nz, nc // 2
        self.local, self.samples = local, per_owner * self.n
        self.chunk = local // self.n
        self.pairs = [(k, c) for k in range(nc) for c in range(k, nc)]
        per_x = -(-len(self.pairs) // nx)
        self.per_z = -(-per_x // nz)
        self.owners = -(-per_x // self.per_z)
        self.per_x = self.per_z * self.owners
        self.blocks = nx * self.per_x
        self.strip = TILE // nc


def mix_kernel(
    plan, x_ref, sign_ref, key_ref, out_ref, root_ref, keys_ref, gram_ref, table, work, recv, back, gathered, left, right, parts, from_core,
    from_y, over_y, from_x, from_z, send_sem, recv_sem, y_sem,
):
    nx, nz, n, nc, ny, local = plan.nx, plan.nz, plan.n, plan.nc, plan.ny, plan.local
    scale = 1.0 / math.sqrt(local * n)
    blocks, chunk = sign_ref.shape[0], work.shape[1]
    per_block = TILE // chunk
    me, col = lax.axis_index("row"), lax.axis_index("col")
    mx, mz = lax.div(me, nz), lax.rem(me, nz)
    my, core = lax.div(col, 2), lax.rem(col, 2)
    strip = core * ny + my
    sibling = (me, col + 1 - 2 * core)

    def peer(k):
        dx, m = lax.rem(k, nx), lax.div(k, nx)
        dz = nz + lax.div(m + 1, 2) * (2 * lax.rem(m, 2) - 1)
        return lax.rem(mx + dx, nx) * nz + lax.rem(mz + dz, nz)

    barrier = pltpu.get_barrier_semaphore()

    def greet(k, carry):
        pl.semaphore_signal(barrier, inc=1, device_id=(peer(k), col), device_id_type=MESH)
        return carry

    lax.fori_loop(1, n, greet, 0)
    for d in range(1, nc):
        pl.semaphore_signal(barrier, inc=1, device_id=(me, lax.rem(col + d, nc)), device_id_type=MESH)

    shared = lax.broadcasted_iota(jnp.int32, (TILE, TILE), 0) & lax.broadcasted_iota(jnp.int32, (TILE, TILE), 1)
    shared = shared ^ shared >> 4
    shared = shared ^ shared >> 2
    shared = shared ^ shared >> 1
    hadamard = (1 - 2 * (shared & 1)).astype(F32)

    def inner(a, carry):
        signed = (hadamard * sign_ref[pl.ds(a, 1), :]).astype(BF16)
        rows = x_ref[pl.ds(pl.multiple_of(a * TILE, TILE), TILE), :]
        work[pl.ds(a * per_block, per_block)] = exact_dot(signed, rows).reshape(per_block, chunk, TILE)
        return carry

    lax.fori_loop(0, blocks, inner, 0)

    def outer(b, carry):
        part, at = lax.div(b * 8, chunk), pl.multiple_of(lax.rem(b * 8, chunk), 8)
        mixed = butterfly([work[a * per_block + part, pl.ds(at, 8), :] for a in range(blocks)])
        for a in range(blocks):
            work[a * per_block + part, pl.ds(at, 8), :] = mixed[a]
        return carry

    lax.fori_loop(0, TILE // 8, outer, 0)
    pl.semaphore_wait(barrier, n + nc - 2)

    def send(src, dst, device, which, arrival=None):
        pltpu.make_async_remote_copy(
            src_ref=src, dst_ref=dst, send_sem=send_sem.at[which],
            recv_sem=recv_sem.at[which] if arrival is None else arrival,
            device_id=device, device_id_type=MESH,
        ).start()

    def there(k, carry):
        device = (peer(k), col)
        send(key_ref, keys_ref.at[me], device, 0)
        send(work.at[device[0]], recv.at[me], device, 1)
        return carry

    lax.fori_loop(1, n, there, 0)
    keys_ref[me] = key_ref[...]
    recv[me] = work[me]

    per_col = n // nc
    rows = per_col * plan.chunk
    wait_for(keys_ref.at[pl.ds(0, n - 1)], recv_sem.at[0])
    bins = lax.broadcasted_iota(jnp.int32, (rows, TILE), 0)

    def count(o, total):
        key = keys_ref[o]
        holder, offset = key // local - col * per_col, key % local - me * plan.chunk
        here = (holder >= 0) & (holder < per_col) & (offset >= 0) & (offset < plan.chunk)
        where = jnp.where(here, holder * plan.chunk + offset, -1)
        return total + jnp.where(bins == where, 1.0, 0.0)

    counts = jnp.sum(lax.fori_loop(0, n, count, jnp.zeros((rows, TILE), F32)), axis=1, keepdims=True)
    wait_for(recv.at[pl.ds(0, n - 1)], recv_sem.at[1])
    radix = min(8, n)

    def low(g, carry):
        mixed = butterfly([recv[radix * g + i] for i in range(radix)])
        for i in range(radix):
            recv[radix * g + i] = mixed[i]
        return carry

    def high(i, carry):
        mixed = butterfly([recv[radix * g + i] for g in range(n // radix)])
        for g in range(n // radix):
            back[radix * g + i] = mixed[g] * scale
        return carry

    lax.fori_loop(0, n // radix, low, 0)
    lax.fori_loop(0, radix, high, 0)

    for d in range(1, nc):
        to = lax.rem(col + d, nc)
        send(back.at[pl.ds(to * per_col, per_col)], gathered.at[col], (me, to), 3)

    out_ref[me] = back[me]
    gathered[col] = back[pl.ds(col * per_col, per_col)]
    wait_for(gathered.at[pl.ds(0, nc - 1)], recv_sem.at[3])

    for c in range(nc):
        here = gathered[c].reshape(rows, TILE)
        right[:, c * TILE:(c + 1) * TILE] = right_parts(here)
        left[c * TILE:(c + 1) * TILE, :] = left_parts((here * counts).T)
    for first in range(0, nc, 2):
        wide = jnp.dot(left[:(first + 2) * TILE, :], right[:, first * TILE:(first + 2) * TILE], preferred_element_type=F32)
        for c in (first, first + 1):
            for k in range(c + 1):
                block = wide[k * TILE:(k + 1) * TILE, (c - first) * TILE:(c - first + 1) * TILE]
                parts[:, plan.pairs.index((k, c))] = block.reshape(nc, plan.strip, TILE)

    send(parts.at[pl.ds((1 - core) * ny, ny)], from_core, sibling, 4)
    wait_for(from_core, recv_sem.at[4])

    def pair(q, carry):
        over_y[q] = parts[core * ny + q] + from_core[q]
        return carry

    lax.fori_loop(0, ny, pair, 0)
    for d in range(1, ny):
        to = lax.rem(my + d, ny)
        send(over_y.at[to], from_y.at[my], (me, to * 2 + core), 5)
    from_y[my] = over_y[my]
    if ny > 1:
        wait_for(from_y.at[pl.ds(0, ny - 1)], recv_sem.at[5])
    own = over_y.at[my]
    total = from_y[0]
    for q in range(1, ny):
        total = total + from_y[q]
    if ny > 1:
        wait_for(over_y.at[pl.ds(0, ny - 1)], send_sem.at[5])
    over_y[my] = total

    def share(q):
        return own.at[pl.ds(q * plan.per_x, plan.per_x)]

    for d in range(1, nx):
        to = lax.rem(mx + d, nx)
        send(share(to), from_x.at[mx], (to * nz + mz, col), 6)
    from_x[mx] = over_y[my, pl.ds(mx * plan.per_x, plan.per_x)]
    wait_for(from_x.at[pl.ds(0, nx - 1)], recv_sem.at[6])
    total = from_x[0]
    for q in range(1, nx):
        total = total + from_x[q]
    wait_for(from_x.at[pl.ds(0, nx - 1)], send_sem.at[6])
    from_x[mx] = total
    slot = plan.per_z

    def piece(ref, q):
        return ref.at[pl.ds(q * slot, slot)]

    for q in range(plan.owners):
        @pl.when(mz != q)
        def _():
            send(piece(from_x.at[mx], q), from_z.at[mz], (mx * nz + q, col), 7)

    @pl.when(mz < plan.owners)
    def _():
        from_z[mz] = from_x[mx, pl.ds(mz * slot, slot)]
        wait_for(from_z.at[pl.ds(0, nz - 1)], recv_sem.at[7])
        total = from_z[0]
        for q in range(1, nz):
            total = total + from_z[q]
        gram_ref[strip, pl.ds(mx * plan.per_x + mz * slot, slot)] = total * (1.0 / plan.samples)
        mine = gram_ref.at[strip, pl.ds(mx * plan.per_x + mz * slot, slot)]
        for d in range(1, nz):
            send(mine, mine, (mx * nz + lax.rem(mz + d, nz), col), 8)
        if plan.owners > 1:
            wait_for(gram_ref.at[strip, pl.ds(0, plan.per_x - slot)], recv_sem.at[8])

    @pl.when(mz >= plan.owners)
    def _():
        other = gram_ref.at[strip, pl.ds(mx * plan.per_x, plan.per_x)]
        wait_for(other, recv_sem.at[8])

    mine = gram_ref.at[strip, pl.ds(mx * plan.per_x, plan.per_x)]
    for d in range(1, nx):
        send(mine, mine, (lax.rem(mx + d, nx) * nz + mz, col), 9)
    wait_for(gram_ref.at[strip, pl.ds(0, plan.blocks - plan.per_x)], recv_sem.at[9])
    mine = gram_ref.at[strip]
    send(mine, mine, sibling, 11)
    for d in range(1, ny):
        send(mine, mine, (me, lax.rem(my + d, ny) * 2 + core), 10, y_sem.at[my])
    for d in range(1, ny):
        q = lax.rem(my + d, ny)
        other = gram_ref.at[core * ny + q]
        wait_for(other, y_sem.at[q])
        send(other, other, sibling, 11)
    def home(k, carry):
        device = peer(k)
        send(back.at[device], out_ref.at[me], (device, col), 2)
        return carry

    lax.fori_loop(1, n, home, 0)
    wait_for(gram_ref.at[pl.ds(0, ny)], recv_sem.at[11])

    def block(k, c):
        return gram_ref[:, plan.pairs.index((k, c))].reshape(TILE, TILE)

    root_of(nc, block, col, root_ref, table, left, right)

    wait_for(out_ref.at[pl.ds(0, n - 1)], recv_sem.at[2])
    wait_for(keys_ref.at[pl.ds(0, n - 1)], send_sem.at[0])
    wait_for(recv.at[pl.ds(0, n - 1)], send_sem.at[1])
    wait_for(out_ref.at[pl.ds(0, n - 1)], send_sem.at[2])
    wait_for(gathered.at[pl.ds(0, nc - 1)], send_sem.at[3])
    wait_for(from_core, send_sem.at[4])
    @pl.when(mz < plan.owners)
    def _():
        if plan.owners > 1:
            wait_for(from_x.at[0, pl.ds(0, (plan.owners - 1) * slot)], send_sem.at[7])
        wait_for(from_z.at[pl.ds(0, nz - 1)], send_sem.at[8])

    @pl.when(mz >= plan.owners)
    def _():
        wait_for(from_x.at[0], send_sem.at[7])

    wait_for(gram_ref.at[strip, pl.ds(0, plan.blocks - plan.per_x)], send_sem.at[9])
    if ny > 1:
        wait_for(gram_ref.at[pl.ds(0, ny - 1)], send_sem.at[10])
    wait_for(gram_ref.at[pl.ds(0, ny)], send_sem.at[11])


def per_device(nx, nz, nc, slab_rows, row_flips, sample_holder, sample_offset):
    local, width = slab_rows.shape
    per_owner = sample_offset.shape[0]
    plan = Plan(nx, nz, nc, local, per_owner)
    n, ny, chunk, strip = plan.n, plan.ny, plan.chunk, plan.strip
    rows = n // nc * chunk
    vmem = pl.BlockSpec(memory_space=pltpu.VMEM)
    signs = (1 - 2 * row_flips).astype(F32).reshape(local // TILE, TILE)
    key = (sample_holder[:, 0] * local + sample_offset).reshape(1, per_owner)

    def buffer(*shape, dtype=F32):
        return pltpu.VMEM(shape, dtype)

    mixed, precond = pl.pallas_call(
        functools.partial(mix_kernel, plan),
        out_shape=(
            jax.ShapeDtypeStruct((n, chunk, width), F32),
            jax.ShapeDtypeStruct((nc * TILE, width), F32),
        ),
        in_specs=[vmem] * 3,
        out_specs=(vmem, vmem),
        scratch_shapes=[
            buffer(n, 1, per_owner, dtype=jnp.int32),
            buffer(nc, plan.blocks, strip, TILE),
            buffer(nc * TILE, nc * TILE),
            buffer(n, chunk, width),
            buffer(n, chunk, width),
            buffer(n, chunk, width),
            buffer(nc, n // nc, chunk, width),
            buffer(nc * TILE, 6 * rows, dtype=BF16),
            buffer(6 * rows, nc * TILE, dtype=BF16),
            buffer(nc, plan.blocks, strip, TILE),
            buffer(ny, plan.blocks, strip, TILE),
            buffer(ny, plan.blocks, strip, TILE),
            buffer(ny, plan.blocks, strip, TILE),
            buffer(nx, plan.per_x, strip, TILE),
            buffer(nz, plan.per_z, strip, TILE),
            pltpu.SemaphoreType.DMA((12,)),
            pltpu.SemaphoreType.DMA((12,)),
            pltpu.SemaphoreType.DMA((ny,)),
        ],
        compiler_params=pltpu.CompilerParams(collective_id=0, has_side_effects=True, vmem_limit_bytes=48 * 2**20),
        name="mix",
    )(slab_rows, signs, key)

    return (mixed.reshape(local, width), precond)


def solution(mesh):
    nx = 4
    nz = mesh.shape["row"] // nx
    in_specs = (P("row", "col"), P("row"), P("row", None), P("row"))
    out_specs = (P("row", "col"), P(None, "col"))
    return jax.shard_map(
        functools.partial(per_device, nx, nz, mesh.shape["col"]),
        mesh=mesh, in_specs=in_specs, out_specs=out_specs, check_vma=False,
    )
```

```python
import functools
import math

import jax
import jax.numpy as jnp
from jax import lax
from jax.experimental import pallas as pl
from jax.experimental.pallas import tpu as pltpu
from jax.sharding import PartitionSpec as P

MESH = pl.DeviceIdType.MESH
F32, BF16 = jnp.float32, jnp.bfloat16
TILE = 128


def split_three(values):
    high = values.astype(BF16)
    rest = values - high.astype(F32)
    middle = rest.astype(BF16)
    return high, middle, (rest - middle.astype(F32)).astype(BF16)


def exact_dot(left, values):
    return sum(jnp.dot(left, part, preferred_element_type=F32) for part in split_three(values))


def butterfly(items):
    items, apart = list(items), 1
    while apart < len(items):
        for i in range(len(items)):
            if not i & apart:
                items[i], items[i + apart] = items[i] + items[i + apart], items[i] - items[i + apart]
        apart *= 2
    return items


def wait_for(ref, sem):
    pltpu.make_async_copy(ref, ref, sem).wait()


def left_parts(values):
    high, middle, low = split_three(values)
    return jnp.concatenate([high, high, middle, middle, high, low], axis=1)


def right_parts(values):
    high, middle, low = split_three(values)
    return jnp.concatenate([high, middle, high, middle, low, high], axis=0)


def factor(block):
    sub = lax.broadcasted_iota(jnp.int32, (8, TILE), 0)
    lane = lax.broadcasted_iota(jnp.int32, (8, TILE), 1)
    row = lax.broadcasted_iota(jnp.int32, (TILE, TILE), 0)
    s, e = block, jnp.where(row == lax.broadcasted_iota(jnp.int32, (TILE, TILE), 1), 1.0, 0.0)
    upper, inverse = [], []
    for t in range(TILE // 8):
        rows = s.shape[0]
        cols = [jnp.broadcast_to(s[:, 8 * t + j:8 * t + j + 1], (rows, TILE)) for j in range(8)]
        pivots = jnp.zeros((8, TILE), F32)
        for j in range(8):
            pivot = jnp.broadcast_to(cols[j][j:j + 1], (8, TILE))
            pivots = jnp.where(sub == j, pivot, pivots)
            r = pltpu.reciprocal(pivot, approx=True)
            m = jnp.where(row[:rows] > j, cols[j], 0.0) * r[0:1]
            for l in range(j + 1, 8):
                cols[l] = cols[l] - m * cols[l][j:j + 1]
            s, e = s - m * s[j:j + 1], e - m * e[j:j + 1]
        root = lax.rsqrt(pivots)
        upper.append(jnp.where(lane >= sub + 8 * t, s[:8] * root, 0.0))
        inverse.append(e[:8] * root)
        s, e = s[8:], e[8:]
    return jnp.concatenate(upper, axis=0), jnp.concatenate(inverse, axis=0)


def root_of(nc, load, mc, out_ref, table, left, right):
    for k in range(nc):
        for c in range(k, nc):
            table[k * TILE:(k + 1) * TILE, c * TILE:(c + 1) * TILE] = load(k, c)

    def step(i, carry):
        at = pl.ds(pl.multiple_of(i * TILE, TILE), TILE)
        upper, inverse = factor(table[at, at])
        out_ref[at, :] = jnp.where(mc == i, upper, 0.0)
        first = left_parts(inverse)
        for k in range(nc - 1):
            @pl.when(i == k)
            def _():
                end = (k + 1) * TILE
                row = jnp.dot(first, right_parts(table[k * TILE:end, end:]), preferred_element_type=F32)
                right[:6 * TILE, end:] = right_parts(row)
                for c in range(k + 1, nc):
                    block = row[:, (c - k - 1) * TILE:(c - k) * TILE]
                    left[c * TILE:(c + 1) * TILE, :6 * TILE] = left_parts(block.T)

                    @pl.when(mc == c)
                    def _():
                        out_ref[k * TILE:end, :] = block
                for c in range((k + 1) // 2 * 2, nc, 2):
                    cols = slice(max(c, k + 1) * TILE, (c + 2) * TILE)
                    rows = slice(end, (c + 2) * TILE)
                    table[rows, cols] = table[rows, cols] - jnp.dot(
                        left[rows, :6 * TILE], right[:6 * TILE, cols], preferred_element_type=F32
                    )
        return carry

    lax.fori_loop(0, nc, step, 0)


class Plan:
    def __init__(self, nx, nz, nc, local, per_owner):
        self.nx, self.nz, self.nc, self.n, self.ny = nx, nz, nc, nx * nz, nc // 2
        self.local, self.samples = local, per_owner * self.n
        self.chunk = local // self.n
        self.pairs = [(k, c) for k in range(nc) for c in range(k, nc)]
        per_x = -(-len(self.pairs) // nx)
        self.per_z = -(-per_x // nz)
        self.owners = -(-per_x // self.per_z)
        self.per_x = self.per_z * self.owners
        cuts = [self.owners * i // 3 for i in range(4)]
        self.spans = [(low, high) for low, high in zip(cuts, cuts[1:]) if high > low]
        self.blocks = nx * self.per_x
        self.strip = TILE // nc


def mix_kernel(
    plan, x_ref, flip_ref, holder_ref, offset_ref, out_ref, root_ref, keys_ref, gram_ref, table, work, recv, back, gathered, left, right, parts, from_core,
    over_y, from_plane, summed, from_z, send_sem, recv_sem,
):
    nx, nz, n, nc, ny, local = plan.nx, plan.nz, plan.n, plan.nc, plan.ny, plan.local
    scale = 1.0 / math.sqrt(local * n)
    blocks, chunk = flip_ref.shape[0], work.shape[1]
    per_block = TILE // chunk
    me, col = lax.axis_index("row"), lax.axis_index("col")
    mx, mz = lax.div(me, nz), lax.rem(me, nz)
    my, core = lax.div(col, 2), lax.rem(col, 2)
    strip = core * ny + my
    sibling = (me, col + 1 - 2 * core)

    def peer(k):
        dx, m = lax.rem(k, nx), lax.div(k, nx)
        dz = nz + lax.div(m + 1, 2) * (2 * lax.rem(m, 2) - 1)
        return lax.rem(mx + dx, nx) * nz + lax.rem(mz + dz, nz)

    barrier = pltpu.get_barrier_semaphore()

    def greet(k, carry):
        pl.semaphore_signal(barrier, inc=1, device_id=(peer(k), col), device_id_type=MESH)
        return carry

    lax.fori_loop(1, n, greet, 0)
    for d in range(1, nc):
        pl.semaphore_signal(barrier, inc=1, device_id=(me, lax.rem(col + d, nc)), device_id_type=MESH)

    shared = lax.broadcasted_iota(jnp.int32, (TILE, TILE), 0) & lax.broadcasted_iota(jnp.int32, (TILE, TILE), 1)
    shared = shared ^ shared >> 4
    shared = shared ^ shared >> 2
    shared = shared ^ shared >> 1
    hadamard = (1 - 2 * (shared & 1)).astype(F32)

    def inner(a, carry):
        signed = (hadamard * (1 - 2 * flip_ref[pl.ds(a, 1), :]).astype(F32)).astype(BF16)
        rows = x_ref[pl.ds(pl.multiple_of(a * TILE, TILE), TILE), :]
        work[pl.ds(a * per_block, per_block)] = exact_dot(signed, rows).reshape(per_block, chunk, TILE)
        return carry

    lax.fori_loop(0, blocks, inner, 0)

    def outer(b, carry):
        part, at = lax.div(b * 8, chunk), pl.multiple_of(lax.rem(b * 8, chunk), 8)
        mixed = butterfly([work[a * per_block + part, pl.ds(at, 8), :] for a in range(blocks)])
        for a in range(blocks):
            work[a * per_block + part, pl.ds(at, 8), :] = mixed[a]
        return carry

    lax.fori_loop(0, TILE // 8, outer, 0)
    pl.semaphore_wait(barrier, n + nc - 2)

    def send(src, dst, device, which):
        pltpu.make_async_remote_copy(
            src_ref=src, dst_ref=dst, send_sem=send_sem.at[which], recv_sem=recv_sem.at[which],
            device_id=device, device_id_type=MESH,
        ).start()

    def there(k, carry):
        device = (peer(k), col)
        send(keys_ref.at[me], keys_ref.at[me], device, 0)
        send(work.at[device[0]], recv.at[me], device, 1)
        return carry

    keys_ref[me] = holder_ref[...] * local + offset_ref[...]
    lax.fori_loop(1, n, there, 0)
    recv[me] = work[me]

    per_col = n // nc
    rows = per_col * plan.chunk
    wait_for(keys_ref.at[pl.ds(0, n - 1)], recv_sem.at[0])
    bins = lax.broadcasted_iota(jnp.int32, (rows, TILE), 0)

    def count(o, total):
        key = keys_ref[o]
        holder, offset = key // local - col * per_col, key % local - me * plan.chunk
        here = (holder >= 0) & (holder < per_col) & (offset >= 0) & (offset < plan.chunk)
        where = jnp.where(here, holder * plan.chunk + offset, -1)
        return total + jnp.where(bins == where, 1.0, 0.0)

    counts = jnp.sum(lax.fori_loop(0, n, count, jnp.zeros((rows, TILE), F32)), axis=1, keepdims=True)
    wait_for(recv.at[pl.ds(0, n - 1)], recv_sem.at[1])
    radix = min(8, n)

    def low(g, carry):
        mixed = butterfly([recv[radix * g + i] for i in range(radix)])
        for i in range(radix):
            recv[radix * g + i] = mixed[i]
        return carry

    def high(i, carry):
        mixed = butterfly([recv[radix * g + i] for g in range(n // radix)])
        for g in range(n // radix):
            back[radix * g + i] = mixed[g] * scale
        return carry

    lax.fori_loop(0, n // radix, low, 0)
    lax.fori_loop(0, radix, high, 0)

    for d in range(1, nc):
        to = lax.rem(col + d, nc)
        send(back.at[pl.ds(to * per_col, per_col)], gathered.at[col], (me, to), 3)

    out_ref[me] = back[me]
    gathered[col] = back[pl.ds(col * per_col, per_col)]
    wait_for(gathered.at[pl.ds(0, nc - 1)], recv_sem.at[3])

    for c in range(nc):
        here = gathered[c].reshape(rows, TILE)
        right[:, c * TILE:(c + 1) * TILE] = right_parts(here)
        left[c * TILE:(c + 1) * TILE, :] = left_parts((here * counts).T)
    for first in range(0, nc, 2):
        wide = jnp.dot(left[:(first + 2) * TILE, :], right[:, first * TILE:(first + 2) * TILE], preferred_element_type=F32)
        for c in (first, first + 1):
            for k in range(c + 1):
                block = wide[k * TILE:(k + 1) * TILE, (c - first) * TILE:(c - first + 1) * TILE]
                parts[:, plan.pairs.index((k, c))] = block.reshape(nc, plan.strip, TILE)

    send(parts.at[pl.ds((1 - core) * ny, ny)], from_core, sibling, 4)
    wait_for(from_core, recv_sem.at[4])

    def pair(q, carry):
        over_y[q] = parts[core * ny + q] + from_core[q]
        return carry

    lax.fori_loop(0, ny, pair, 0)
    plane = nx * ny

    def across(d):
        to_x, to_y = lax.rem(mx + d // ny, nx), lax.rem(my + d % ny, ny)
        return to_x, to_y, (to_x * nz + mz, to_y * 2 + core)

    slot = plan.per_z

    def span(p, x=None):
        low, high = plan.spans[p]
        return pl.ds((0 if x is None else x * plan.per_x) + low * slot, (high - low) * slot)

    def owner(p):
        return (mz >= plan.spans[p][0]) & (mz < plan.spans[p][1])

    stages = range(len(plan.spans))
    for p in stages:
        for d in range(1, plane):
            to_x, to_y, device = across(d)
            send(over_y.at[to_y, span(p, to_x)], from_plane.at[mx * ny + my, span(p)], device, 9 + p)
    from_plane[mx * ny + my] = over_y[my, pl.ds(mx * plan.per_x, plan.per_x)]
    for p in stages:
        wait_for(from_plane.at[pl.ds(0, plane - 1), span(p)], recv_sem.at[9 + p])
        total = from_plane[0, span(p)]
        for q in range(1, plane):
            total = total + from_plane[q, span(p)]
        summed[span(p)] = total
        for q in range(*plan.spans[p]):
            @pl.when(mz != q)
            def _():
                send(summed.at[pl.ds(q * slot, slot)], from_z.at[mz], (mx * nz + q, col), 12 + p)
    for p in stages:
        @pl.when(owner(p))
        def _():
            from_z[mz] = summed[pl.ds(mz * slot, slot)]
            wait_for(from_z.at[pl.ds(0, nz - 1)], recv_sem.at[12 + p])
            total = from_z[0]
            for q in range(1, nz):
                total = total + from_z[q]
            gram_ref[strip, pl.ds(mx * plan.per_x + mz * slot, slot)] = total * (1.0 / plan.samples)
            mine = gram_ref.at[strip, pl.ds(mx * plan.per_x + mz * slot, slot)]
            for d in range(1, nz):
                send(mine, mine, (mx * nz + lax.rem(mz + d, nz), col), 15 + p)

    def all_but_own(p, sem):
        low, high = plan.spans[p]

        @pl.when(owner(p))
        def _():
            if high - low > 1:
                wait_for(summed.at[pl.ds(0, (high - low - 1) * slot)], sem)

        @pl.when(jnp.logical_not(owner(p)))
        def _():
            wait_for(summed.at[pl.ds(0, (high - low) * slot)], sem)

    for p in stages:
        all_but_own(p, recv_sem.at[15 + p])
        mine = gram_ref.at[strip, span(p, mx)]
        for d in range(1, plane):
            send(mine, mine, across(d)[2], 18 + p)
    for p in stages:
        wait_for(from_plane.at[pl.ds(0, plane - 1), span(p)], recv_sem.at[18 + p])
        for x in range(nx):
            mine = gram_ref.at[pl.ds(core * ny, ny), span(p, x)]
            send(mine, mine, sibling, 5)

    def home(k, carry):
        device = peer(k)
        send(back.at[device], out_ref.at[me], (device, col), 2)
        return carry

    lax.fori_loop(1, n, home, 0)
    wait_for(gram_ref.at[pl.ds(0, ny)], recv_sem.at[5])

    def block(k, c):
        return gram_ref[:, plan.pairs.index((k, c))].reshape(TILE, TILE)

    root_of(nc, block, col, root_ref, table, left, right)

    wait_for(out_ref.at[pl.ds(0, n - 1)], recv_sem.at[2])
    wait_for(keys_ref.at[pl.ds(0, n - 1)], send_sem.at[0])
    wait_for(recv.at[pl.ds(0, n - 1)], send_sem.at[1])
    wait_for(out_ref.at[pl.ds(0, n - 1)], send_sem.at[2])
    wait_for(gathered.at[pl.ds(0, nc - 1)], send_sem.at[3])
    wait_for(from_core, send_sem.at[4])
    for p in stages:
        wait_for(from_plane.at[pl.ds(0, plane - 1), span(p)], send_sem.at[9 + p])
        all_but_own(p, send_sem.at[12 + p])

        @pl.when(owner(p))
        def _():
            wait_for(from_z.at[pl.ds(0, nz - 1)], send_sem.at[15 + p])

        wait_for(from_plane.at[pl.ds(0, plane - 1), span(p)], send_sem.at[18 + p])
    wait_for(gram_ref.at[pl.ds(0, ny)], send_sem.at[5])


def per_device(nx, nz, nc, slab_rows, row_flips, sample_holder, sample_offset):
    local, width = slab_rows.shape
    per_owner = sample_offset.shape[0]
    plan = Plan(nx, nz, nc, local, per_owner)
    n, ny, chunk, strip = plan.n, plan.ny, plan.chunk, plan.strip
    rows = n // nc * chunk
    vmem = pl.BlockSpec(memory_space=pltpu.VMEM)
    def buffer(*shape, dtype=F32):
        return pltpu.VMEM(shape, dtype)

    mixed, precond = pl.pallas_call(
        functools.partial(mix_kernel, plan),
        out_shape=(
            jax.ShapeDtypeStruct((n, chunk, width), F32),
            jax.ShapeDtypeStruct((nc * TILE, width), F32),
        ),
        in_specs=[vmem] * 4,
        out_specs=(vmem, vmem),
        scratch_shapes=[
            buffer(n, 1, per_owner, dtype=jnp.int32),
            buffer(nc, plan.blocks, strip, TILE),
            buffer(nc * TILE, nc * TILE),
            buffer(n, chunk, width),
            buffer(n, chunk, width),
            buffer(n, chunk, width),
            buffer(nc, n // nc, chunk, width),
            buffer(nc * TILE, 6 * rows, dtype=BF16),
            buffer(6 * rows, nc * TILE, dtype=BF16),
            buffer(nc, plan.blocks, strip, TILE),
            buffer(ny, plan.blocks, strip, TILE),
            buffer(ny, plan.blocks, strip, TILE),
            buffer(nx * ny, plan.per_x, strip, TILE),
            buffer(plan.per_x, strip, TILE),
            buffer(nz, plan.per_z, strip, TILE),
            pltpu.SemaphoreType.DMA((21,)),
            pltpu.SemaphoreType.DMA((21,)),
        ],
        compiler_params=pltpu.CompilerParams(collective_id=0, has_side_effects=True, vmem_limit_bytes=48 * 2**20),
        name="mix",
    )(slab_rows, row_flips.reshape(local // TILE, TILE), sample_holder.reshape(1, per_owner), sample_offset.reshape(1, per_owner))

    return (mixed.reshape(local, width), precond)


def solution(mesh):
    nx = 4
    nz = mesh.shape["row"] // nx
    in_specs = (P("row", "col"), P("row"), P("row", None), P("row"))
    out_specs = (P("row", "col"), P(None, "col"))
    return jax.shard_map(
        functools.partial(per_device, nx, nz, mesh.shape["col"]),
        mesh=mesh, in_specs=in_specs, out_specs=out_specs, check_vma=False,
    )
```

```python
import functools
import math

import jax
import jax.numpy as jnp
from jax import lax
from jax.experimental import pallas as pl
from jax.experimental.pallas import tpu as pltpu
from jax.sharding import PartitionSpec as P

MESH = pl.DeviceIdType.MESH
F32, BF16 = jnp.float32, jnp.bfloat16
TILE = 128


def split_three(values):
    high = values.astype(BF16)
    rest = values - high.astype(F32)
    middle = rest.astype(BF16)
    return high, middle, (rest - middle.astype(F32)).astype(BF16)


def exact_dot(left, values):
    return sum(jnp.dot(left, part, preferred_element_type=F32) for part in split_three(values))


def butterfly(items):
    items, apart = list(items), 1
    while apart < len(items):
        for i in range(len(items)):
            if not i & apart:
                items[i], items[i + apart] = items[i] + items[i + apart], items[i] - items[i + apart]
        apart *= 2
    return items


def wait_for(ref, sem):
    pltpu.make_async_copy(ref, ref, sem).wait()


def left_parts(values):
    high, middle, low = split_three(values)
    return jnp.concatenate([high, high, middle, middle, high, low], axis=1)


def right_parts(values):
    high, middle, low = split_three(values)
    return jnp.concatenate([high, middle, high, middle, low, high], axis=0)


def factor(block):
    sub = lax.broadcasted_iota(jnp.int32, (8, TILE), 0)
    lane = lax.broadcasted_iota(jnp.int32, (8, TILE), 1)
    row = lax.broadcasted_iota(jnp.int32, (TILE, TILE), 0)
    s, e = block, jnp.where(row == lax.broadcasted_iota(jnp.int32, (TILE, TILE), 1), 1.0, 0.0)
    upper, inverse = [], []
    for t in range(TILE // 8):
        rows = s.shape[0]
        cols = [jnp.broadcast_to(s[:, 8 * t + j:8 * t + j + 1], (rows, TILE)) for j in range(8)]
        pivots = jnp.zeros((8, TILE), F32)
        for j in range(8):
            pivot = jnp.broadcast_to(cols[j][j:j + 1], (8, TILE))
            pivots = jnp.where(sub == j, pivot, pivots)
            r = pltpu.reciprocal(pivot, approx=True)
            m = jnp.where(row[:rows] > j, cols[j], 0.0) * r[0:1]
            for l in range(j + 1, 8):
                cols[l] = cols[l] - m * cols[l][j:j + 1]
            s, e = s - m * s[j:j + 1], e - m * e[j:j + 1]
        root = lax.rsqrt(pivots)
        upper.append(jnp.where(lane >= sub + 8 * t, s[:8] * root, 0.0))
        inverse.append(e[:8] * root)
        s, e = s[8:], e[8:]
    return jnp.concatenate(upper, axis=0), jnp.concatenate(inverse, axis=0)


def root_of(nc, load, mc, out_ref, table, left, right):
    for k in range(nc):
        for c in range(k, nc):
            table[k * TILE:(k + 1) * TILE, c * TILE:(c + 1) * TILE] = load(k, c)

    def step(i, carry):
        at = pl.ds(pl.multiple_of(i * TILE, TILE), TILE)
        upper, inverse = factor(table[at, at])
        out_ref[at, :] = jnp.where(mc == i, upper, 0.0)
        first = left_parts(inverse)
        for k in range(nc - 1):
            @pl.when(i == k)
            def _():
                end = (k + 1) * TILE
                row = jnp.dot(first, right_parts(table[k * TILE:end, end:]), preferred_element_type=F32)
                right[:6 * TILE, end:] = right_parts(row)
                for c in range(k + 1, nc):
                    block = row[:, (c - k - 1) * TILE:(c - k) * TILE]
                    left[c * TILE:(c + 1) * TILE, :6 * TILE] = left_parts(block.T)

                    @pl.when(mc == c)
                    def _():
                        out_ref[k * TILE:end, :] = block
                for c in range((k + 1) // 2 * 2, nc, 2):
                    cols = slice(max(c, k + 1) * TILE, (c + 2) * TILE)
                    rows = slice(end, (c + 2) * TILE)
                    table[rows, cols] = table[rows, cols] - jnp.dot(
                        left[rows, :6 * TILE], right[:6 * TILE, cols], preferred_element_type=F32
                    )
        return carry

    lax.fori_loop(0, nc, step, 0)


class Plan:
    def __init__(self, nx, nz, nc, local, per_owner):
        self.nx, self.nz, self.nc, self.n, self.ny = nx, nz, nc, nx * nz, nc // 2
        self.local, self.samples = local, per_owner * self.n
        self.chunk = local // self.n
        self.pairs = [(k, c) for k in range(nc) for c in range(k, nc)]
        per_x = -(-len(self.pairs) // nx)
        self.per_z = -(-per_x // nz)
        self.owners = -(-per_x // self.per_z)
        self.per_x = self.per_z * self.owners
        cuts = [self.owners * i // 3 for i in range(4)]
        self.spans = [(low, high) for low, high in zip(cuts, cuts[1:]) if high > low]
        self.blocks = nx * self.per_x
        self.strip = TILE // nc


def mix_kernel(
    plan, x_ref, flip_ref, holder_ref, offset_ref, out_ref, root_ref, keys_ref, gram_ref, table, work, recv, back, gathered, left, right, parts, from_core,
    over_y, from_plane, summed, from_z, send_sem, recv_sem,
):
    nx, nz, n, nc, ny, local = plan.nx, plan.nz, plan.n, plan.nc, plan.ny, plan.local
    scale = 1.0 / math.sqrt(local * n)
    blocks, chunk = flip_ref.shape[0], work.shape[1]
    per_block = TILE // chunk
    me, col = lax.axis_index("row"), lax.axis_index("col")
    mx, mz = lax.div(me, nz), lax.rem(me, nz)
    my, core = lax.div(col, 2), lax.rem(col, 2)
    strip = core * ny + my
    sibling = (me, col + 1 - 2 * core)

    def peer(k):
        dx, m = lax.rem(k, nx), lax.div(k, nx)
        dz = nz + lax.div(m + 1, 2) * (2 * lax.rem(m, 2) - 1)
        return lax.rem(mx + dx, nx) * nz + lax.rem(mz + dz, nz)

    barrier = pltpu.get_barrier_semaphore()

    def greet(k, carry):
        pl.semaphore_signal(barrier, inc=1, device_id=(peer(k), col), device_id_type=MESH)
        return carry

    lax.fori_loop(1, n, greet, 0)
    for d in range(1, nc):
        pl.semaphore_signal(barrier, inc=1, device_id=(me, lax.rem(col + d, nc)), device_id_type=MESH)

    shared = lax.broadcasted_iota(jnp.int32, (TILE, TILE), 0) & lax.broadcasted_iota(jnp.int32, (TILE, TILE), 1)
    shared = shared ^ shared >> 4
    shared = shared ^ shared >> 2
    shared = shared ^ shared >> 1
    hadamard = (1 - 2 * (shared & 1)).astype(F32)

    def inner(a, carry):
        signed = (hadamard * (1 - 2 * flip_ref[pl.ds(a, 1), :]).astype(F32)).astype(BF16)
        rows = x_ref[pl.ds(pl.multiple_of(a * TILE, TILE), TILE), :]
        work[pl.ds(a * per_block, per_block)] = exact_dot(signed, rows).reshape(per_block, chunk, TILE)
        return carry

    lax.fori_loop(0, blocks, inner, 0)

    def outer(b, carry):
        part, at = lax.div(b * 8, chunk), pl.multiple_of(lax.rem(b * 8, chunk), 8)
        mixed = butterfly([work[a * per_block + part, pl.ds(at, 8), :] for a in range(blocks)])
        for a in range(blocks):
            work[a * per_block + part, pl.ds(at, 8), :] = mixed[a]
        return carry

    lax.fori_loop(0, TILE // 8, outer, 0)
    pl.semaphore_wait(barrier, n + nc - 2)

    def send(src, dst, device, which):
        pltpu.make_async_remote_copy(
            src_ref=src, dst_ref=dst, send_sem=send_sem.at[which], recv_sem=recv_sem.at[which],
            device_id=device, device_id_type=MESH,
        ).start()

    def there(k, carry):
        device = (peer(k), col)
        send(keys_ref.at[me], keys_ref.at[me], device, 0)
        return carry

    half = plan.chunk // 2

    def there_half(k, carry, h):
        device = peer(k)
        send(work.at[device, pl.ds(h * half, half)], recv.at[me, pl.ds(h * half, half)], (device, col), 1 if h == 0 else 7)
        return carry

    keys_ref[me] = holder_ref[...] * local + offset_ref[...]
    lax.fori_loop(1, n, there, 0)
    for h in range(2):
        lax.fori_loop(1, n, functools.partial(there_half, h=h), 0)
    recv[me] = work[me]

    per_col = n // nc
    rows = per_col * plan.chunk
    wait_for(keys_ref.at[pl.ds(0, n - 1)], recv_sem.at[0])
    bins = lax.broadcasted_iota(jnp.int32, (rows, TILE), 0)

    def count(o, total):
        key = keys_ref[o]
        holder, offset = key // local - col * per_col, key % local - me * plan.chunk
        here = (holder >= 0) & (holder < per_col) & (offset >= 0) & (offset < plan.chunk)
        where = jnp.where(here, holder * plan.chunk + offset, -1)
        return total + jnp.where(bins == where, 1.0, 0.0)

    counts = jnp.sum(lax.fori_loop(0, n, count, jnp.zeros((rows, TILE), F32)), axis=1, keepdims=True)
    radix = min(8, n)

    def low(g, carry, rows_of):
        mixed = butterfly([recv[radix * g + i, rows_of] for i in range(radix)])
        for i in range(radix):
            recv[radix * g + i, rows_of] = mixed[i]
        return carry

    def high(i, carry, rows_of):
        mixed = butterfly([recv[radix * g + i, rows_of] for g in range(n // radix)])
        for g in range(n // radix):
            back[radix * g + i, rows_of] = mixed[g] * scale
        return carry

    for h in range(2):
        rows_of = pl.ds(h * half, half)
        wait_for(recv.at[pl.ds(0, n - 1), rows_of], recv_sem.at[1 if h == 0 else 7])
        lax.fori_loop(0, n // radix, functools.partial(low, rows_of=rows_of), 0)
        lax.fori_loop(0, radix, functools.partial(high, rows_of=rows_of), 0)
        for d in range(1, nc):
            to = lax.rem(col + d, nc)
            send(back.at[pl.ds(to * per_col, per_col), rows_of], gathered.at[col, pl.ds(0, per_col), rows_of], (me, to), 3 if h == 0 else 8)

    def home(k, carry):
        device = peer(k)
        send(back.at[device], out_ref.at[me], (device, col), 2)
        return carry

    early = n // 4
    lax.fori_loop(n - early, n, home, 0)
    out_ref[me] = back[me]
    gathered[col] = back[pl.ds(col * per_col, per_col)]
    wait_for(gathered.at[pl.ds(0, nc - 1), pl.ds(0, per_col), pl.ds(0, half)], recv_sem.at[3])
    wait_for(gathered.at[pl.ds(0, nc - 1), pl.ds(0, per_col), pl.ds(0, half)], recv_sem.at[8])

    for c in range(nc):
        here = gathered[c].reshape(rows, TILE)
        right[:, c * TILE:(c + 1) * TILE] = right_parts(here)
        left[c * TILE:(c + 1) * TILE, :] = left_parts((here * counts).T)
    for first in range(0, nc, 2):
        wide = jnp.dot(left[:(first + 2) * TILE, :], right[:, first * TILE:(first + 2) * TILE], preferred_element_type=F32)
        for c in (first, first + 1):
            for k in range(c + 1):
                block = wide[k * TILE:(k + 1) * TILE, (c - first) * TILE:(c - first + 1) * TILE]
                parts[:, plan.pairs.index((k, c))] = block.reshape(nc, plan.strip, TILE)

    send(parts.at[pl.ds((1 - core) * ny, ny)], from_core, sibling, 4)
    wait_for(from_core, recv_sem.at[4])

    def pair(q, carry):
        over_y[q] = parts[core * ny + q] + from_core[q]
        return carry

    lax.fori_loop(0, ny, pair, 0)
    plane = nx * ny

    def across(d):
        to_x, to_y = lax.rem(mx + d // ny, nx), lax.rem(my + d % ny, ny)
        return to_x, to_y, (to_x * nz + mz, to_y * 2 + core)

    slot = plan.per_z

    def span(p, x=None):
        low, high = plan.spans[p]
        return pl.ds((0 if x is None else x * plan.per_x) + low * slot, (high - low) * slot)

    def owner(p):
        return (mz >= plan.spans[p][0]) & (mz < plan.spans[p][1])

    stages = range(len(plan.spans))
    for p in stages:
        for d in range(1, plane):
            to_x, to_y, device = across(d)
            send(over_y.at[to_y, span(p, to_x)], from_plane.at[mx * ny + my, span(p)], device, 9 + p)
    from_plane[mx * ny + my] = over_y[my, pl.ds(mx * plan.per_x, plan.per_x)]
    for p in stages:
        wait_for(from_plane.at[pl.ds(0, plane - 1), span(p)], recv_sem.at[9 + p])
        total = from_plane[0, span(p)]
        for q in range(1, plane):
            total = total + from_plane[q, span(p)]
        summed[span(p)] = total
        for q in range(*plan.spans[p]):
            @pl.when(mz != q)
            def _():
                send(summed.at[pl.ds(q * slot, slot)], from_z.at[mz], (mx * nz + q, col), 12 + p)
    for p in stages:
        @pl.when(owner(p))
        def _():
            from_z[mz] = summed[pl.ds(mz * slot, slot)]
            wait_for(from_z.at[pl.ds(0, nz - 1)], recv_sem.at[12 + p])
            total = from_z[0]
            for q in range(1, nz):
                total = total + from_z[q]
            gram_ref[strip, pl.ds(mx * plan.per_x + mz * slot, slot)] = total * (1.0 / plan.samples)
            mine = gram_ref.at[strip, pl.ds(mx * plan.per_x + mz * slot, slot)]
            for d in range(1, nz):
                send(mine, mine, (mx * nz + lax.rem(mz + d, nz), col), 15 + p)

    def all_but_own(p, sem):
        low, high = plan.spans[p]

        @pl.when(owner(p))
        def _():
            if high - low > 1:
                wait_for(summed.at[pl.ds(0, (high - low - 1) * slot)], sem)

        @pl.when(jnp.logical_not(owner(p)))
        def _():
            wait_for(summed.at[pl.ds(0, (high - low) * slot)], sem)

    for p in stages:
        all_but_own(p, recv_sem.at[15 + p])
        mine = gram_ref.at[strip, span(p, mx)]
        for d in range(1, plane):
            send(mine, mine, across(d)[2], 18 + p)
    for p in stages:
        wait_for(from_plane.at[pl.ds(0, plane - 1), span(p)], recv_sem.at[18 + p])
        for x in range(nx):
            mine = gram_ref.at[pl.ds(core * ny, ny), span(p, x)]
            send(mine, mine, sibling, 5)

    lax.fori_loop(1, n - early, home, 0)
    wait_for(gram_ref.at[pl.ds(0, ny)], recv_sem.at[5])

    def block(k, c):
        return gram_ref[:, plan.pairs.index((k, c))].reshape(TILE, TILE)

    root_of(nc, block, col, root_ref, table, left, right)

    wait_for(out_ref.at[pl.ds(0, n - 1)], recv_sem.at[2])
    wait_for(keys_ref.at[pl.ds(0, n - 1)], send_sem.at[0])
    wait_for(recv.at[pl.ds(0, n - 1), pl.ds(0, half)], send_sem.at[1])
    wait_for(recv.at[pl.ds(0, n - 1), pl.ds(0, half)], send_sem.at[7])
    wait_for(out_ref.at[pl.ds(0, n - 1)], send_sem.at[2])
    wait_for(gathered.at[pl.ds(0, nc - 1), pl.ds(0, per_col), pl.ds(0, half)], send_sem.at[3])
    wait_for(gathered.at[pl.ds(0, nc - 1), pl.ds(0, per_col), pl.ds(0, half)], send_sem.at[8])
    wait_for(from_core, send_sem.at[4])
    for p in stages:
        wait_for(from_plane.at[pl.ds(0, plane - 1), span(p)], send_sem.at[9 + p])
        all_but_own(p, send_sem.at[12 + p])

        @pl.when(owner(p))
        def _():
            wait_for(from_z.at[pl.ds(0, nz - 1)], send_sem.at[15 + p])

        wait_for(from_plane.at[pl.ds(0, plane - 1), span(p)], send_sem.at[18 + p])
    wait_for(gram_ref.at[pl.ds(0, ny)], send_sem.at[5])


def per_device(nx, nz, nc, slab_rows, row_flips, sample_holder, sample_offset):
    local, width = slab_rows.shape
    per_owner = sample_offset.shape[0]
    plan = Plan(nx, nz, nc, local, per_owner)
    n, ny, chunk, strip = plan.n, plan.ny, plan.chunk, plan.strip
    rows = n // nc * chunk
    vmem = pl.BlockSpec(memory_space=pltpu.VMEM)
    def buffer(*shape, dtype=F32):
        return pltpu.VMEM(shape, dtype)

    mixed, precond = pl.pallas_call(
        functools.partial(mix_kernel, plan),
        out_shape=(
            jax.ShapeDtypeStruct((n, chunk, width), F32),
            jax.ShapeDtypeStruct((nc * TILE, width), F32),
        ),
        in_specs=[vmem] * 4,
        out_specs=(vmem, vmem),
        scratch_shapes=[
            buffer(n, 1, per_owner, dtype=jnp.int32),
            buffer(nc, plan.blocks, strip, TILE),
            buffer(nc * TILE, nc * TILE),
            buffer(n, chunk, width),
            buffer(n, chunk, width),
            buffer(n, chunk, width),
            buffer(nc, n // nc, chunk, width),
            buffer(nc * TILE, 6 * rows, dtype=BF16),
            buffer(6 * rows, nc * TILE, dtype=BF16),
            buffer(nc, plan.blocks, strip, TILE),
            buffer(ny, plan.blocks, strip, TILE),
            buffer(ny, plan.blocks, strip, TILE),
            buffer(nx * ny, plan.per_x, strip, TILE),
            buffer(plan.per_x, strip, TILE),
            buffer(nz, plan.per_z, strip, TILE),
            pltpu.SemaphoreType.DMA((21,)),
            pltpu.SemaphoreType.DMA((21,)),
        ],
        compiler_params=pltpu.CompilerParams(collective_id=0, has_side_effects=True, vmem_limit_bytes=48 * 2**20),
        name="mix",
    )(slab_rows, row_flips.reshape(local // TILE, TILE), sample_holder.reshape(1, per_owner), sample_offset.reshape(1, per_owner))

    return (mixed.reshape(local, width), precond)


def solution(mesh):
    nx = 4
    nz = mesh.shape["row"] // nx
    in_specs = (P("row", "col"), P("row"), P("row", None), P("row"))
    out_specs = (P("row", "col"), P(None, "col"))
    return jax.shard_map(
        functools.partial(per_device, nx, nz, mesh.shape["col"]),
        mesh=mesh, in_specs=in_specs, out_specs=out_specs, check_vma=False,
    )
```
